512 devices in a mesh: ctx: 128 (over z, x, y_lo), head: 4 (over y_hi, core).
Axes of the slice: x: 4, y: 8 (y_hi: 2, y_lo: 4; y = y_hi * 4 + y_lo), z: 8, core: 2. Of those that a mesh axis runs over, the one named last changes fastest.
Arguments:
- q_nope: bfloat16 [32768, 8192], P('ctx', 'head'), may hold values from -6 to 6
- q_rope: bfloat16 [32768, 4096], P('ctx', 'head'), may hold values from -200 to 200
- latent: bfloat16 [32768, 512], P(('ctx', 'head')), may hold values from -6 to 6
- k_rope: bfloat16 [32768, 64], P(('ctx', 'head')), may hold values from -4 to 4
- blocks: int32 [128, 2], replicated, may hold values from 0 to 255, as said below
- w_uk: bfloat16 [512, 8192], P('ctx', 'head'), may hold values from -0.25 to 0.25
- w_uv: bfloat16 [512, 8192], P('ctx', 'head'), may hold values from -0.25 to 0.25
Outputs:
- attended: bfloat16 [32768, 8192], P('ctx', 'head')
The draws below stay inside these ranges and needn't reach their ends.
Inputs may be any that keep to these rules, and one draw needn't show every extreme that they name: `blocks`: row c holds two block numbers b and 255 - b; the first column is a permutation of 0 to 127.
All inputs are finite; a program needn't handle non-finite values.
Results may differ from the reference program's by a relative error of at most 0.017.
Values may be sent and summed in bfloat16 or wider, within the bound.
No kernel may reach another device: no remote copies, remote signals or barrier semaphores. Data moves between devices by JAX's collectives and lax.ppermute only.
A program may use at most 64 MiB of HBM per device.

```python
import jax
import jax.numpy as jnp
from jax import lax

LAT = 512
ROPE = 64
NOPE = 128
VDIM = 128
TOK_DEV = 256
STEPS = 3
HEADS = 64
TOKENS = 32768
N_CTX = 128


def rope_base(key):
    return jnp.clip(jax.random.normal(key, (TOKENS, ROPE), jnp.float32), -4.0, 4.0)


def draw_k_rope(key, part):
    base = rope_base(key)
    return base.astype(jnp.bfloat16)


def draw_q_rope(key, part):
    key = jax.random.fold_in(key, 23)
    values = jnp.clip(jax.random.normal(key, (TOKENS, HEADS * ROPE), jnp.float32), -6.0, 6.0)
    return values.astype(jnp.bfloat16)


def draw_blocks(key, part):
    key = jax.random.fold_in(key, 37)
    order = jax.random.permutation(key, N_CTX).astype(jnp.int32)
    return jnp.stack([order, 2 * N_CTX - 1 - order], axis=1).astype(jnp.int32)


def shard_levels(rng, dims, split, smallest, high):
    factor_of = 1.0
    for axis_at, shards_of in split:
        steps = jax.random.uniform(jax.random.fold_in(jax.random.fold_in(rng, 6), axis_at), (shards_of,), jnp.float32, smallest / len(split), high / len(split))
        factor_of = factor_of * jnp.repeat(jnp.exp(steps), dims[axis_at] // shards_of).reshape((-1,) + (1,) * (len(dims) - 1 - axis_at))
    return factor_of


def centred(key, shape, scale, limit, split=(), kind=jnp.bfloat16):
    gain = shard_levels(key, shape, split, -0.22, 0.18) if split else 1.0
    drawn = jax.random.normal(key, shape, jnp.float32) * scale * gain
    return jnp.minimum(jnp.maximum(drawn, -limit), limit).astype(kind)


def setup_inputs(seed: int = 0) -> dict:
    streams_of = jax.random.split(jax.random.key(seed), 8)
    return {
        "q_nope": centred(streams_of[0], (TOKENS, HEADS * NOPE), 1.0, 6.0, ((0, 128), (1, 4))),
        "q_rope": draw_q_rope(jax.random.fold_in(streams_of[7], 71), 0),
        "latent": centred(streams_of[2], (TOKENS, LAT), 1.0, 6.0, ((0, 512),)),
        "k_rope": draw_k_rope(jax.random.fold_in(streams_of[7], 71), 0),
        "blocks": draw_blocks(jax.random.fold_in(streams_of[7], 71), 0),
        "w_uk": centred(streams_of[5], (LAT, HEADS * NOPE), LAT ** -0.5, 0.25, ((0, 128), (1, 4))),
        "w_uv": centred(streams_of[6], (LAT, HEADS * VDIM), LAT ** -0.5, 0.25, ((0, 128), (1, 4))),
    }


def angles_of(pos, width):
    half = width // 2
    freq = 10000.0 ** (-(2.0 * jnp.arange(half, dtype=jnp.float32)) / width)
    return pos.astype(jnp.float32)[..., None] * freq


def rotate(values, angles):
    half = values.shape[-1] // 2
    first = values[..., :half]
    second = values[..., half:]
    cosine = jnp.cos(angles)
    sine = jnp.sin(angles)
    return jnp.concatenate([first * cosine - second * sine, first * sine + second * cosine], axis=-1)


def reference(q_nope, q_rope, latent, k_rope, blocks, w_uk, w_uv):
    half = TOK_DEV // 2
    rows = jnp.arange(TOKENS, dtype=jnp.int32)
    shard_of = rows // TOK_DEV
    local = rows % TOK_DEV
    block_id = jnp.where(local < half, blocks[shard_of, 0], blocks[shard_of, 1])
    pos = (block_id * half + local % half).astype(jnp.int32)
    k_rot = rotate(k_rope.astype(jnp.float32), angles_of(pos, ROPE)).astype(jnp.bfloat16)
    keys = jnp.dot(latent, w_uk, preferred_element_type=jnp.float32)
    values = jnp.dot(latent, w_uv, preferred_element_type=jnp.float32)
    scale = 1.0 / (NOPE + ROPE) ** 0.5
    highest = lax.Precision.HIGHEST

    def one_shard(index):
        start = index * TOK_DEV
        query_n = lax.dynamic_slice_in_dim(q_nope, start, TOK_DEV, 0).astype(jnp.float32).reshape(TOK_DEV, HEADS, NOPE)
        query_r = lax.dynamic_slice_in_dim(q_rope, start, TOK_DEV, 0).astype(jnp.float32).reshape(TOK_DEV, HEADS, ROPE)
        query_pos = lax.dynamic_slice_in_dim(pos, start, TOK_DEV, 0)
        query_rot = rotate(query_r, angles_of(query_pos, ROPE)[:, None, :])
        starts = [(((index - step) % N_CTX) * TOK_DEV).astype(jnp.int32) for step in range(STEPS)]
        key_n = jnp.concatenate([lax.dynamic_slice_in_dim(keys, s, TOK_DEV, 0) for s in starts], 0)
        key_v = jnp.concatenate([lax.dynamic_slice_in_dim(values, s, TOK_DEV, 0) for s in starts], 0)
        key_r = jnp.concatenate([lax.dynamic_slice_in_dim(k_rot, s, TOK_DEV, 0) for s in starts], 0)
        key_pos = jnp.concatenate([lax.dynamic_slice_in_dim(pos, s, TOK_DEV, 0) for s in starts], 0)
        count = key_n.shape[0]
        score_n = jnp.einsum("thn,khn->htk", query_n, key_n.reshape(count, HEADS, NOPE), precision=highest)
        score_r = jnp.einsum("thr,kr->htk", query_rot, key_r.astype(jnp.float32), precision=highest)
        scores = (score_n + score_r) * scale
        allowed = (key_pos[None, :] <= query_pos[:, None])[None, :, :]
        masked = jnp.where(allowed, scores, -jnp.inf)
        peak = jnp.max(masked, axis=-1, keepdims=True)
        probs = jnp.exp(masked - peak)
        total = jnp.sum(probs, axis=-1)
        weights = probs.astype(jnp.bfloat16)
        summed = jnp.einsum("htk,khv->thv", weights.astype(jnp.float32), key_v.reshape(count, HEADS, VDIM), precision=highest)
        result = summed / jnp.transpose(total)[:, :, None]
        return result.reshape(TOK_DEV, HEADS * VDIM).astype(jnp.bfloat16)

    shards = lax.map(one_shard, jnp.arange(N_CTX, dtype=jnp.int32))
    return shards.reshape(TOKENS, HEADS * VDIM)
```

```python
import functools

import jax
import jax.numpy as jnp
from jax import lax
from jax.experimental import pallas as pl
from jax.experimental.pallas import tpu as pltpu
from jax.sharding import PartitionSpec as P

ROPE = 64
NOPE = 128
VDIM = 128
STEPS = 3
NZ, NX, NY = 8, 4, 4
HALF = 128
LOG2E = 1.4426950408889634
NEG = -1e30


def place(z, x, y):
    return ((z % NZ) * NX + x % NX) * NY + y


def shifted(value, dz, dx):
    pairs = [
        (place(z, x, y), place(z + dz, x + dx, y))
        for z in range(NZ)
        for x in range(NX)
        for y in range(NY)
    ]
    return lax.ppermute(value, "ctx", pairs)


def members(plan, colour):
    if plan == 0:
        return [(z, (colour - 2 * z) % NX) for z in range(NZ)]
    return [((colour - 2 * x) % 4 + 4 * far, x) for x in range(NX) for far in range(2)]


def colour_groups(plan):
    return [[place(z, x, y) for z, x in members(plan, c) for y in range(NY)] for c in range(4)]


def colour_of(plan, z, x):
    return (x + 2 * z) % 4 if plan == 0 else (z + 2 * x) % 4


def gather_pieces(plan, shard):
    groups = colour_groups(plan)
    size = len(groups[0])
    own = lax.all_to_all(
        jnp.broadcast_to(shard[None], (size,) + shard.shape), "ctx", 0, 0, axis_index_groups=groups
    ).reshape(size * shard.shape[0], shard.shape[1])
    mid = own.shape[0] // 2
    if plan == 0:
        up, down = (0, -1), (0, 1)
        side, other = (-1, 0), (1, 0)
    else:
        up, down = (-1, 0), (1, 0)
        side, other = (0, -1), (0, 1)
    return (
        own,
        shifted(own, *up),
        shifted(own, *down),
        shifted(own[:mid], *side),
        shifted(own[mid:], *other),
    )


def row_order(plan, z, x, rows):
    at = jnp.arange(NZ * NX * NY * rows, dtype=jnp.int32)
    quarter = at.shape[0] // 4
    piece, rest = at // quarter, at % quarter
    step = jnp.where(piece < 2, piece, 5 - piece)
    colour = (colour_of(plan, z, x) + step) % 4
    member, inner = rest // (NY * rows), rest % (NY * rows)
    if plan == 0:
        mz = member
        mx = (colour - 2 * mz) % 4
    else:
        mx = member // 2
        mz = (colour - 2 * mx) % 4 + 4 * (member % 2)
    return (mz * NX + mx) * (NY * rows) + inner


def angles_of(pos, width):
    half = width // 2
    freq = 10000.0 ** (-(2.0 * jnp.arange(half, dtype=jnp.float32)) / width)
    return pos.astype(jnp.float32)[..., None] * freq


def rotate(values, angles):
    half = values.shape[-1] // 2
    first = values[..., :half]
    second = values[..., half:]
    cosine = jnp.cos(angles)
    sine = jnp.sin(angles)
    return jnp.concatenate(
        [first * cosine - second * sine, first * sine + second * cosine], axis=-1
    )


def shard_positions(pair, start, count, tok_len):
    rows = start + jnp.arange(count, dtype=jnp.int32)
    half = tok_len // 2
    block_id = jnp.where(rows < half, pair[0], pair[1])
    return block_id * half + rows % half


def rotate_queries_kernel(x_ref, cos_ref, sin_ref, o_ref):
    lane = lax.broadcasted_iota(jnp.int32, cos_ref.shape, 1)
    low = lane % 64 < 32
    left = lane < 64
    cosine = cos_ref[...]
    sine = sin_ref[...]
    for pair in range(x_ref.shape[1] // 128):
        x = x_ref[:, pair * 128 : (pair + 1) * 128].astype(jnp.float32)
        swapped = jnp.where(low, pltpu.roll(x, 96, 1), pltpu.roll(x, 32, 1))
        turned = x * cosine + swapped * sine
        high = turned.astype(jnp.bfloat16).astype(jnp.float32)
        rest = turned - high
        first = jnp.where(left, high, pltpu.roll(rest, 64, 1))
        second = jnp.where(left, pltpu.roll(high, 64, 1), rest)
        o_ref[:, pair * 256 : pair * 256 + 128] = first.astype(jnp.bfloat16)
        o_ref[:, pair * 256 + 128 : pair * 256 + 256] = second.astype(jnp.bfloat16)


def rotate_queries(q_rope, angles):
    tok_len, width = q_rope.shape
    cosine = jnp.cos(angles)
    sine = jnp.sin(angles)
    cos4 = jnp.concatenate([cosine] * 4, 1)
    sin4 = jnp.concatenate([-sine, sine, -sine, sine], 1)
    return pl.pallas_call(
        rotate_queries_kernel,
        out_shape=jax.ShapeDtypeStruct((tok_len, 2 * width), jnp.bfloat16),
        cost_estimate=pl.CostEstimate(
            flops=4 * tok_len * width, bytes_accessed=6 * tok_len * width, transcendentals=0
        ),
        name="rotate_queries",
    )(q_rope, cos4, sin4)


def attend_kernel(width, pieces, sel_ref, lat_ref, rot_ref, qn_ref, qr_ref, *refs):
    k_refs, v_refs = refs[:pieces], refs[pieces : 2 * pieces]
    o_ref, key_s, val_s = refs[-3:]
    lat = lat_ref[...]
    up_k = jnp.concatenate([r[...] for r in k_refs], 0)
    up_v = jnp.concatenate([r[...] for r in v_refs], 0)
    key_s[...] = jnp.dot(lat, up_k, preferred_element_type=jnp.float32).astype(jnp.bfloat16)
    val_s[...] = jnp.dot(lat, up_v, preferred_element_type=jnp.float32).astype(jnp.bfloat16)
    coef = LOG2E / (NOPE + ROPE) ** 0.5
    row = lax.broadcasted_iota(jnp.int32, (HALF, HALF), 0)
    col = lax.broadcasted_iota(jnp.int32, (HALF, HALF), 1)
    causal = col <= row
    contract = (((1,), (1,)), ((), ()))
    early = [sel_ref[j] != 0 for j in range(STEPS - 1)]
    q_at = [pl.multiple_of(jnp.where(e, 0, HALF), HALF) for e in early]
    k_at = [
        pl.multiple_of(jnp.where(e, j + 1, STEPS + j + 1) * HALF, HALF)
        for j, e in enumerate(early)
    ]

    for h in range(width):
        cols = slice(h * NOPE, (h + 1) * NOPE)

        def queries(start):
            rows = pl.ds(start, HALF)
            return jnp.concatenate([qn_ref[rows, cols], qr_ref[rows, cols]], 1)

        def scores(q, start, count):
            rows = pl.ds(start, count)
            k = jnp.concatenate([key_s[rows, cols], rot_ref[rows, :]], 1)
            return lax.dot_general(q, k, contract, preferred_element_type=jnp.float32)

        q_late = queries(HALF)
        full = scores(q_late, 0, (STEPS + 1) * HALF)
        late = [full[:, i * HALF : (i + 1) * HALF] for i in range(STEPS)]
        late.append(jnp.where(causal, full[:, STEPS * HALF :], NEG))
        first = jnp.where(causal, scores(queries(0), 0, HALF), NEG)
        chosen = [scores(queries(q_at[j]), k_at[j], HALF) for j in range(STEPS - 1)]

        top_late = functools.reduce(jnp.maximum, late)
        top_first = first
        for e, s in zip(early, chosen):
            top_late = jnp.maximum(top_late, jnp.where(e, NEG, s))
            top_first = jnp.maximum(top_first, jnp.where(e, s, NEG))
        top_late = jnp.max(top_late, axis=1, keepdims=True)
        top_first = jnp.max(top_first, axis=1, keepdims=True)
        p_late = [jnp.exp2((s - top_late) * coef) for s in late]
        p_first = jnp.exp2((first - top_first) * coef)
        p_chosen = [
            jnp.exp2((s - jnp.where(e, top_first, top_late)) * coef)
            for e, s in zip(early, chosen)
        ]
        sum_late = functools.reduce(jnp.add, p_late)
        sum_first = p_first
        for e, p in zip(early, p_chosen):
            sum_late = sum_late + jnp.where(e, 0.0, p)
            sum_first = sum_first + jnp.where(e, p, 0.0)
        sum_late = jnp.sum(sum_late, axis=1, keepdims=True)
        sum_first = jnp.sum(sum_first, axis=1, keepdims=True)

        def weighted(p, start, count):
            return jnp.dot(
                p.astype(jnp.bfloat16),
                val_s[pl.ds(start, count), cols],
                preferred_element_type=jnp.float32,
            )

        out_late = weighted(jnp.concatenate(p_late, 1), 0, (STEPS + 1) * HALF)
        out_first = weighted(p_first, 0, HALF)
        for j, e in enumerate(early):
            part = weighted(p_chosen[j], k_at[j], HALF)
            out_late = out_late + jnp.where(e, 0.0, part)
            out_first = out_first + jnp.where(e, part, 0.0)
        o_ref[:HALF, cols] = (out_first / sum_first).astype(jnp.bfloat16)
        o_ref[HALF:, cols] = (out_late / sum_late).astype(jnp.bfloat16)


def attend(lane, lanes, sel, lat, rot, q_nope, q_rot, pieces, earlier):
    tok_len, all_cols = q_nope.shape
    lane_cols = all_cols // lanes
    width = 2
    cols = width * NOPE
    steps = lane_cols // cols
    count, depth = lat.shape

    def whole(shape):
        return pl.BlockSpec(shape, lambda i: (0, 0))

    def mine(shape):
        return pl.BlockSpec(shape, lambda i: (0, lane * steps + i))

    in_specs = [
        pl.BlockSpec(memory_space=pltpu.SMEM),
        whole(lat.shape),
        whole(rot.shape),
        mine((tok_len, cols)),
        mine((tok_len, cols)),
    ]
    in_specs += [pl.BlockSpec((p.shape[0], cols), lambda i: (0, i)) for p in pieces]
    in_specs += [pl.BlockSpec((p.shape[0], cols), lambda i: (0, steps + i)) for p in pieces]
    operands = [sel, lat, rot, q_nope, q_rot, *pieces, *pieces]
    aliases = {}
    if earlier is not None:
        in_specs.append(pl.BlockSpec(memory_space=pl.ANY))
        aliases = {len(operands): 0}
        operands.append(earlier)
    heads = lane_cols // NOPE
    flops = 4 * count * depth * lane_cols + heads * 7 * HALF * HALF * (2 * 256 + 2 * VDIM)
    return pl.pallas_call(
        functools.partial(attend_kernel, width, len(pieces)),
        grid=(steps,),
        in_specs=in_specs,
        out_specs=mine((tok_len, cols)),
        out_shape=jax.ShapeDtypeStruct((tok_len, all_cols), jnp.bfloat16),
        scratch_shapes=[
            pltpu.VMEM((count, cols), jnp.bfloat16),
            pltpu.VMEM((count, cols), jnp.bfloat16),
        ],
        input_output_aliases=aliases,
        compiler_params=pltpu.CompilerParams(vmem_limit_bytes=40 * 1024 * 1024),
        cost_estimate=pl.CostEstimate(
            flops=flops,
            bytes_accessed=2 * (4 * depth * lane_cols + 3 * tok_len * lane_cols + count * 640),
            transcendentals=heads * 7 * HALF * HALF,
        ),
        name=f"attend_{lane}",
    )(*operands)


def local(q_nope, q_rope, latent, k_rope, blocks, w_uk, w_uv):
    tok_len, all_cols = q_nope.shape
    quarter = latent.shape[0]
    w_rows = w_uk.shape[0]
    n_ctx = lax.axis_size("ctx")
    ctx_index = lax.axis_index("ctx")
    head_index = lax.axis_index("head")
    z, x = ctx_index // (NX * NY), (ctx_index // NY) % NX
    lanes = 2
    lane_cols = all_cols // lanes

    pieces = []
    for lane in range(lanes):
        cols = slice(lane * lane_cols, (lane + 1) * lane_cols)
        shard = jnp.concatenate([w_uk[:, cols], w_uv[:, cols]], 1)
        pieces.append(gather_pieces(lane, shard))

    own_pair = blocks[ctx_index]
    own_pos = shard_positions(own_pair, head_index * quarter, quarter, tok_len)
    own_rot = rotate(k_rope.astype(jnp.float32), angles_of(own_pos, ROPE)).astype(jnp.bfloat16)
    own = jnp.concatenate([latent, own_rot, own_rot], 1)
    across = lax.ppermute(own, "head", [(0, 2), (2, 0), (1, 3), (3, 1)])
    upper = head_index // 2 == 0
    two = jnp.stack([jnp.where(upper, own, across), jnp.where(upper, across, own)])
    visited = [two]
    for step in range(1, STEPS):
        pairs = [(source, (source + step) % n_ctx) for source in range(n_ctx)]
        visited.append(lax.ppermute(two, "ctx", pairs))
    held = jnp.stack(visited)
    both = lax.all_gather(held, "head", axis=0, axis_index_groups=[[0, 1], [2, 3]])
    both = both.transpose(2, 1, 0, 3, 4).reshape(STEPS * tok_len, own.shape[1])
    depth = latent.shape[1]
    lat_all, rot_all = both[:, :depth], both[:, depth:]

    lats = []
    for lane in range(lanes):
        order = row_order(lane, z, x, w_rows)
        place_of = lax.broadcasted_iota(jnp.int32, (depth, depth), 0) == order[None, :]
        lats.append(jnp.dot(lat_all, place_of.astype(jnp.bfloat16)))

    query_pos = shard_positions(own_pair, 0, tok_len, tok_len)
    q_rot = rotate_queries(q_rope, angles_of(query_pos, ROPE))
    sel = jnp.stack(
        [
            (blocks[(ctx_index - step) % n_ctx, 0] < own_pair[0]).astype(jnp.int32)
            for step in range(1, STEPS)
        ]
    )
    result = None
    for lane in range(lanes):
        result = attend(
            lane, lanes, sel, lats[lane], rot_all, q_nope, q_rot, pieces[lane], result
        )
    return result


def solution(mesh):
    in_specs = (
        P("ctx", "head"),
        P("ctx", "head"),
        P(("ctx", "head"), None),
        P(("ctx", "head"), None),
        P(),
        P("ctx", "head"),
        P("ctx", "head"),
    )
    out_specs = P("ctx", "head")
    return jax.shard_map(local, mesh=mesh, in_specs=in_specs, out_specs=out_specs, check_vma=False)
```

```python
import functools

import jax
import jax.numpy as jnp
from jax import lax
from jax.experimental import pallas as pl
from jax.experimental.pallas import tpu as pltpu
from jax.sharding import PartitionSpec as P

ROPE = 64
NOPE = 128
VDIM = 128
STEPS = 3
NZ, NX, NY = 8, 4, 4
N_HEAD = 4
HALF = 128
LOG2E = 1.4426950408889634
NEG = -1e30


def place(z, x, y):
    return ((z % NZ) * NX + x % NX) * NY + y


def members(plan, colour):
    if plan == 0:
        return [(z, (colour - 2 * z) % NX) for z in range(NZ)]
    return [((colour - 2 * x) % 4 + 4 * far, x) for x in range(NX) for far in range(2)]


def plan_of(head):
    return head % 2


def colour_of(plan, z, x):
    return jnp.where(plan == 0, x + 2 * z, z + 2 * x) % 4


def gather_own(shard):
    groups = [
        [place(z, x, y) * N_HEAD + head for z, x in members(plan_of(head), c) for y in range(NY)]
        for head in range(N_HEAD)
        for c in range(4)
    ]
    size = len(groups[0])
    return lax.all_to_all(
        jnp.broadcast_to(shard[None], (size,) + shard.shape),
        ("ctx", "head"),
        0,
        0,
        axis_index_groups=groups,
    ).reshape(size * shard.shape[0], shard.shape[1])


def from_neighbour(value, step, along):
    pairs = []
    for head in range(N_HEAD):
        on_x = (plan_of(head) == 0) == (along == 0)
        dz, dx = (0, step) if on_x else (step, 0)
        pairs += [
            (place(z + dz, x + dx, y) * N_HEAD + head, place(z, x, y) * N_HEAD + head)
            for z in range(NZ)
            for x in range(NX)
            for y in range(NY)
        ]
    return lax.ppermute(value, ("ctx", "head"), pairs)


def gather_rest(own, side):
    return (own, from_neighbour(own, 1, 0), from_neighbour(own, -1, 0), from_neighbour(own, side, 1))


def row_order(plan, z, x, rows):
    at = jnp.arange(NZ * NX * NY * rows, dtype=jnp.int32)
    quarter = at.shape[0] // 4
    piece, rest = at // quarter, at % quarter
    step = jnp.where(piece < 2, piece, 5 - piece)
    colour = (colour_of(plan, z, x) + step) % 4
    member, inner = rest // (NY * rows), rest % (NY * rows)
    mz = jnp.where(plan == 0, member, (colour - 2 * (member // 2)) % 4 + 4 * (member % 2))
    mx = jnp.where(plan == 0, (colour - 2 * member) % 4, member // 2)
    return (mz * NX + mx) * (NY * rows) + inner


def angles_of(pos, width):
    half = width // 2
    freq = 10000.0 ** (-(2.0 * jnp.arange(half, dtype=jnp.float32)) / width)
    return pos.astype(jnp.float32)[..., None] * freq


def rotate(values, angles):
    half = values.shape[-1] // 2
    first = values[..., :half]
    second = values[..., half:]
    cosine = jnp.cos(angles)
    sine = jnp.sin(angles)
    return jnp.concatenate(
        [first * cosine - second * sine, first * sine + second * cosine], axis=-1
    )


def shard_positions(pair, start, count, tok_len):
    rows = start + jnp.arange(count, dtype=jnp.int32)
    half = tok_len // 2
    block_id = jnp.where(rows < half, pair[0], pair[1])
    return block_id * half + rows % half


def rotate_queries_kernel(x_ref, cos_ref, sin_ref, o_ref):
    lane = lax.broadcasted_iota(jnp.int32, cos_ref.shape, 1)
    low = lane % 64 < 32
    left = lane < 64
    cosine = cos_ref[...]
    sine = sin_ref[...]
    for pair in range(x_ref.shape[1] // 128):
        x = x_ref[:, pair * 128 : (pair + 1) * 128].astype(jnp.float32)
        swapped = jnp.where(low, pltpu.roll(x, 96, 1), pltpu.roll(x, 32, 1))
        turned = x * cosine + swapped * sine
        high = turned.astype(jnp.bfloat16).astype(jnp.float32)
        rest = turned - high
        first = jnp.where(left, high, pltpu.roll(rest, 64, 1))
        second = jnp.where(left, pltpu.roll(high, 64, 1), rest)
        o_ref[:, pair * 256 : pair * 256 + 128] = first.astype(jnp.bfloat16)
        o_ref[:, pair * 256 + 128 : pair * 256 + 256] = second.astype(jnp.bfloat16)


def rotate_queries(q_rope, angles):
    tok_len, width = q_rope.shape
    cosine = jnp.cos(angles)
    sine = jnp.sin(angles)
    cos4 = jnp.concatenate([cosine] * 4, 1)
    sin4 = jnp.concatenate([-sine, sine, -sine, sine], 1)
    return pl.pallas_call(
        rotate_queries_kernel,
        out_shape=jax.ShapeDtypeStruct((tok_len, 2 * width), jnp.bfloat16),
        cost_estimate=pl.CostEstimate(
            flops=4 * tok_len * width, bytes_accessed=6 * tok_len * width, transcendentals=0
        ),
        name="rotate_queries",
    )(q_rope, cos4, sin4)


def attend_kernel(width, pieces, sel_ref, lat_ref, rot_ref, qn_ref, qr_ref, *refs):
    k_refs, v_refs = refs[:pieces], refs[pieces : 2 * pieces]
    o_ref, key_s, val_s = refs[-3:]
    lat = lat_ref[...]
    up_k = jnp.concatenate([r[...] for r in k_refs], 0)
    up_v = jnp.concatenate([r[...] for r in v_refs], 0)
    key_s[...] = jnp.dot(lat, up_k, preferred_element_type=jnp.float32).astype(jnp.bfloat16)
    val_s[...] = jnp.dot(lat, up_v, preferred_element_type=jnp.float32).astype(jnp.bfloat16)
    coef = LOG2E / (NOPE + ROPE) ** 0.5
    row = lax.broadcasted_iota(jnp.int32, (HALF, HALF), 0)
    col = lax.broadcasted_iota(jnp.int32, (HALF, HALF), 1)
    causal = col <= row
    contract = (((1,), (1,)), ((), ()))
    early = [sel_ref[j] != 0 for j in range(STEPS - 1)]
    q_at = [pl.multiple_of(jnp.where(e, 0, HALF), HALF) for e in early]
    k_at = [
        pl.multiple_of(jnp.where(e, j + 1, STEPS + j + 1) * HALF, HALF)
        for j, e in enumerate(early)
    ]

    for h in range(width):
        cols = slice(h * NOPE, (h + 1) * NOPE)

        def queries(start):
            rows = pl.ds(start, HALF)
            return jnp.concatenate([qn_ref[rows, cols], qr_ref[rows, cols]], 1)

        def scores(q, start, count):
            rows = pl.ds(start, count)
            k = jnp.concatenate([key_s[rows, cols], rot_ref[rows, :]], 1)
            return lax.dot_general(q, k, contract, preferred_element_type=jnp.float32)

        q_late = queries(HALF)
        full = scores(q_late, 0, (STEPS + 1) * HALF)
        late = [full[:, i * HALF : (i + 1) * HALF] for i in range(STEPS)]
        late.append(jnp.where(causal, full[:, STEPS * HALF :], NEG))
        first = jnp.where(causal, scores(queries(0), 0, HALF), NEG)
        chosen = [scores(queries(q_at[j]), k_at[j], HALF) for j in range(STEPS - 1)]

        top_late = functools.reduce(jnp.maximum, late)
        top_first = first
        for e, s in zip(early, chosen):
            top_late = jnp.maximum(top_late, jnp.where(e, NEG, s))
            top_first = jnp.maximum(top_first, jnp.where(e, s, NEG))
        top_late = jnp.max(top_late, axis=1, keepdims=True)
        top_first = jnp.max(top_first, axis=1, keepdims=True)
        p_late = [jnp.exp2((s - top_late) * coef) for s in late]
        p_first = jnp.exp2((first - top_first) * coef)
        p_chosen = [
            jnp.exp2((s - jnp.where(e, top_first, top_late)) * coef)
            for e, s in zip(early, chosen)
        ]
        sum_late = functools.reduce(jnp.add, p_late)
        sum_first = p_first
        for e, p in zip(early, p_chosen):
            sum_late = sum_late + jnp.where(e, 0.0, p)
            sum_first = sum_first + jnp.where(e, p, 0.0)
        sum_late = jnp.sum(sum_late, axis=1, keepdims=True)
        sum_first = jnp.sum(sum_first, axis=1, keepdims=True)

        def weighted(p, start, count):
            return jnp.dot(
                p.astype(jnp.bfloat16),
                val_s[pl.ds(start, count), cols],
                preferred_element_type=jnp.float32,
            )

        out_late = weighted(jnp.concatenate(p_late, 1), 0, (STEPS + 1) * HALF)
        out_first = weighted(p_first, 0, HALF)
        for j, e in enumerate(early):
            part = weighted(p_chosen[j], k_at[j], HALF)
            out_late = out_late + jnp.where(e, 0.0, part)
            out_first = out_first + jnp.where(e, part, 0.0)
        o_ref[:HALF, cols] = (out_first / sum_first).astype(jnp.bfloat16)
        o_ref[HALF:, cols] = (out_late / sum_late).astype(jnp.bfloat16)


def attend(lane, lanes, sel, lat, rot, q_nope, q_rot, pieces, earlier):
    tok_len, all_cols = q_nope.shape
    lane_cols = all_cols // lanes
    width = 2
    cols = width * NOPE
    steps = lane_cols // cols
    count, depth = lat.shape

    def whole(shape):
        return pl.BlockSpec(shape, lambda i: (0, 0))

    def mine(shape):
        return pl.BlockSpec(shape, lambda i: (0, lane * steps + i))

    in_specs = [
        pl.BlockSpec(memory_space=pltpu.SMEM),
        whole(lat.shape),
        whole(rot.shape),
        mine((tok_len, cols)),
        mine((tok_len, cols)),
    ]
    in_specs += [pl.BlockSpec((p.shape[0], cols), lambda i: (0, i)) for p in pieces]
    in_specs += [pl.BlockSpec((p.shape[0], cols), lambda i: (0, steps + i)) for p in pieces]
    operands = [sel, lat, rot, q_nope, q_rot, *pieces, *pieces]
    aliases = {}
    if earlier is not None:
        in_specs.append(pl.BlockSpec(memory_space=pl.ANY))
        aliases = {len(operands): 0}
        operands.append(earlier)
    heads = lane_cols // NOPE
    flops = 4 * count * depth * lane_cols + heads * 7 * HALF * HALF * (2 * 256 + 2 * VDIM)
    return pl.pallas_call(
        functools.partial(attend_kernel, width, len(pieces)),
        grid=(steps,),
        in_specs=in_specs,
        out_specs=mine((tok_len, cols)),
        out_shape=jax.ShapeDtypeStruct((tok_len, all_cols), jnp.bfloat16),
        scratch_shapes=[
            pltpu.VMEM((count, cols), jnp.bfloat16),
            pltpu.VMEM((count, cols), jnp.bfloat16),
        ],
        input_output_aliases=aliases,
        compiler_params=pltpu.CompilerParams(vmem_limit_bytes=40 * 1024 * 1024),
        cost_estimate=pl.CostEstimate(
            flops=flops,
            bytes_accessed=2 * (4 * depth * lane_cols + 3 * tok_len * lane_cols + count * 640),
            transcendentals=heads * 7 * HALF * HALF,
        ),
        name=f"attend_{lane}",
    )(*operands)


def local(q_nope, q_rope, latent, k_rope, blocks, w_uk, w_uv):
    tok_len, all_cols = q_nope.shape
    quarter = latent.shape[0]
    w_rows = w_uk.shape[0]
    n_ctx = lax.axis_size("ctx")
    ctx_index = lax.axis_index("ctx")
    head_index = lax.axis_index("head")
    z, x = ctx_index // (NX * NY), (ctx_index // NY) % NX
    lanes = 2
    lane_cols = all_cols // lanes

    parts = [slice(lane * lane_cols, (lane + 1) * lane_cols) for lane in range(lanes)]
    shard = jnp.concatenate([w[:, cols] for cols in parts for w in (w_uk, w_uv)], 1)
    own_rows = gather_own(shard)
    pieces = []
    for lane in range(lanes):
        cols = slice(2 * lane * lane_cols, 2 * (lane + 1) * lane_cols)
        pieces.append(gather_rest(own_rows[:, cols], 1 - 2 * (lane % 2)))

    own_pair = blocks[ctx_index]
    own_pos = shard_positions(own_pair, head_index * quarter, quarter, tok_len)
    own_rot = rotate(k_rope.astype(jnp.float32), angles_of(own_pos, ROPE)).astype(jnp.bfloat16)
    own = jnp.concatenate([latent, own_rot, own_rot], 1)
    across = lax.ppermute(own, "head", [(0, 2), (2, 0), (1, 3), (3, 1)])
    upper = head_index // 2 == 0
    two = jnp.stack([jnp.where(upper, own, across), jnp.where(upper, across, own)])
    visited = [two]
    for step in range(1, STEPS):
        pairs = [(source, (source + step) % n_ctx) for source in range(n_ctx)]
        visited.append(lax.ppermute(two, "ctx", pairs))
    held = jnp.stack(visited)
    both = lax.all_gather(held, "head", axis=0, axis_index_groups=[[0, 1], [2, 3]])
    both = both.transpose(2, 1, 0, 3, 4).reshape(STEPS * tok_len, own.shape[1])
    depth = latent.shape[1]
    lat_all, rot_all = both[:, :depth], both[:, depth:]

    order = row_order(plan_of(head_index), z, x, w_rows)
    place_of = lax.broadcasted_iota(jnp.int32, (depth, depth), 0) == order[None, :]
    lat_all = jnp.dot(lat_all, place_of.astype(jnp.bfloat16))

    query_pos = shard_positions(own_pair, 0, tok_len, tok_len)
    q_rot = rotate_queries(q_rope, angles_of(query_pos, ROPE))
    sel = jnp.stack(
        [
            (blocks[(ctx_index - step) % n_ctx, 0] < own_pair[0]).astype(jnp.int32)
            for step in range(1, STEPS)
        ]
    )
    result = None
    for lane in range(lanes):
        result = attend(
            lane, lanes, sel, lat_all, rot_all, q_nope, q_rot, pieces[lane], result
        )
    return result


def solution(mesh):
    in_specs = (
        P("ctx", "head"),
        P("ctx", "head"),
        P(("ctx", "head"), None),
        P(("ctx", "head"), None),
        P(),
        P("ctx", "head"),
        P("ctx", "head"),
    )
    out_specs = P("ctx", "head")
    return jax.shard_map(local, mesh=mesh, in_specs=in_specs, out_specs=out_specs, check_vma=False)
```

```python
import functools

import jax
import jax.numpy as jnp
from jax import lax
from jax.experimental import pallas as pl
from jax.experimental.pallas import tpu as pltpu
from jax.sharding import PartitionSpec as P

ROPE = 64
NOPE = 128
VDIM = 128
STEPS = 3
NZ, NX, NY = 8, 4, 4
N_HEAD = 4
HALF = 128
LOG2E = 1.4426950408889634
NEG = -1e30


def place(z, x, y):
    return ((z % NZ) * NX + x % NX) * NY + y


def members(plan, colour):
    if plan == 0:
        return [(z, (colour - 2 * z) % NX) for z in range(NZ)]
    return [((colour - 2 * x) % 4 + 4 * far, x) for x in range(NX) for far in range(2)]


def plan_of(head):
    return head % 2


def colour_of(plan, z, x):
    return jnp.where(plan == 0, x + 2 * z, z + 2 * x) % 4


def gather_own(shard):
    groups = [
        [place(z, x, y) * N_HEAD + head for z, x in members(plan_of(head), c) for y in range(NY)]
        for head in range(N_HEAD)
        for c in range(4)
    ]
    size = len(groups[0])
    return lax.all_to_all(
        jnp.broadcast_to(shard[None], (size,) + shard.shape),
        ("ctx", "head"),
        0,
        0,
        axis_index_groups=groups,
    ).reshape(size * shard.shape[0], shard.shape[1])


def gather_rest(own):
    groups = []
    for head in range(N_HEAD):
        shift = plan_of(head)
        for z in range(shift, NZ, 2):
            for x in range(shift, NX, 2):
                for y in range(NY):
                    block = [place(z + dz, x + dx, y) for dz in range(2) for dx in range(2)]
                    groups.append([at * N_HEAD + head for at in block])
    return lax.all_to_all(
        jnp.broadcast_to(own[None], (4,) + own.shape),
        ("ctx", "head"),
        0,
        0,
        axis_index_groups=groups,
    )


def row_order(plan, z, x, rows):
    at = jnp.arange(NZ * NX * NY * rows, dtype=jnp.int32)
    quarter = at.shape[0] // 4
    piece, rest = at // quarter, at % quarter
    corner_z, corner_x = z - (z + plan) % 2, x - (x + plan) % 2
    colour = colour_of(plan, corner_z + piece // 2 + NZ, corner_x + piece % 2 + NX)
    member, inner = rest // (NY * rows), rest % (NY * rows)
    mz = jnp.where(plan == 0, member, (colour - 2 * (member // 2)) % 4 + 4 * (member % 2))
    mx = jnp.where(plan == 0, (colour - 2 * member) % 4, member // 2)
    return (mz * NX + mx) * (NY * rows) + inner


def angles_of(pos, width):
    half = width // 2
    freq = 10000.0 ** (-(2.0 * jnp.arange(half, dtype=jnp.float32)) / width)
    return pos.astype(jnp.float32)[..., None] * freq


def rotate(values, angles):
    half = values.shape[-1] // 2
    first = values[..., :half]
    second = values[..., half:]
    cosine = jnp.cos(angles)
    sine = jnp.sin(angles)
    return jnp.concatenate(
        [first * cosine - second * sine, first * sine + second * cosine], axis=-1
    )


def shard_positions(pair, start, count, tok_len):
    rows = start + jnp.arange(count, dtype=jnp.int32)
    half = tok_len // 2
    block_id = jnp.where(rows < half, pair[0], pair[1])
    return block_id * half + rows % half


def rotate_queries_kernel(x_ref, cos_ref, sin_ref, o_ref):
    lane = lax.broadcasted_iota(jnp.int32, cos_ref.shape, 1)
    low = lane % 64 < 32
    left = lane < 64
    cosine = cos_ref[...]
    sine = sin_ref[...]
    for pair in range(x_ref.shape[1] // 128):
        x = x_ref[:, pair * 128 : (pair + 1) * 128].astype(jnp.float32)
        swapped = jnp.where(low, pltpu.roll(x, 96, 1), pltpu.roll(x, 32, 1))
        turned = x * cosine + swapped * sine
        high = turned.astype(jnp.bfloat16).astype(jnp.float32)
        rest = turned - high
        first = jnp.where(left, high, pltpu.roll(rest, 64, 1))
        second = jnp.where(left, pltpu.roll(high, 64, 1), rest)
        o_ref[:, pair * 256 : pair * 256 + 128] = first.astype(jnp.bfloat16)
        o_ref[:, pair * 256 + 128 : pair * 256 + 256] = second.astype(jnp.bfloat16)


def rotate_queries(q_rope, angles):
    tok_len, width = q_rope.shape
    cosine = jnp.cos(angles)
    sine = jnp.sin(angles)
    cos4 = jnp.concatenate([cosine] * 4, 1)
    sin4 = jnp.concatenate([-sine, sine, -sine, sine], 1)
    return pl.pallas_call(
        rotate_queries_kernel,
        out_shape=jax.ShapeDtypeStruct((tok_len, 2 * width), jnp.bfloat16),
        cost_estimate=pl.CostEstimate(
            flops=4 * tok_len * width, bytes_accessed=6 * tok_len * width, transcendentals=0
        ),
        name="rotate_queries",
    )(q_rope, cos4, sin4)


def attend_kernel(width, sel_ref, lat_ref, rot_ref, qn_ref, qr_ref, k_ref, v_ref, *refs):
    o_ref, key_s, val_s = refs[-3:]
    lat = lat_ref[...]
    up_k = k_ref[...].reshape(lat.shape[1], k_ref.shape[2])
    up_v = v_ref[...].reshape(lat.shape[1], v_ref.shape[2])
    key_s[...] = jnp.dot(lat, up_k, preferred_element_type=jnp.float32).astype(jnp.bfloat16)
    val_s[...] = jnp.dot(lat, up_v, preferred_element_type=jnp.float32).astype(jnp.bfloat16)
    coef = LOG2E / (NOPE + ROPE) ** 0.5
    row = lax.broadcasted_iota(jnp.int32, (HALF, HALF), 0)
    col = lax.broadcasted_iota(jnp.int32, (HALF, HALF), 1)
    causal = col <= row
    contract = (((1,), (1,)), ((), ()))
    early = [sel_ref[j] != 0 for j in range(STEPS - 1)]
    q_at = [pl.multiple_of(jnp.where(e, 0, HALF), HALF) for e in early]
    k_at = [
        pl.multiple_of(jnp.where(e, j + 1, STEPS + j + 1) * HALF, HALF)
        for j, e in enumerate(early)
    ]

    for h in range(width):
        cols = slice(h * NOPE, (h + 1) * NOPE)

        def queries(start):
            rows = pl.ds(start, HALF)
            return jnp.concatenate([qn_ref[rows, cols], qr_ref[rows, cols]], 1)

        def scores(q, start, count):
            rows = pl.ds(start, count)
            k = jnp.concatenate([key_s[rows, cols], rot_ref[rows, :]], 1)
            return lax.dot_general(q, k, contract, preferred_element_type=jnp.float32)

        q_late = queries(HALF)
        full = scores(q_late, 0, (STEPS + 1) * HALF)
        late = [full[:, i * HALF : (i + 1) * HALF] for i in range(STEPS)]
        late.append(jnp.where(causal, full[:, STEPS * HALF :], NEG))
        first = jnp.where(causal, scores(queries(0), 0, HALF), NEG)
        chosen = [scores(queries(q_at[j]), k_at[j], HALF) for j in range(STEPS - 1)]

        top_late = functools.reduce(jnp.maximum, late)
        top_first = first
        for e, s in zip(early, chosen):
            top_late = jnp.maximum(top_late, jnp.where(e, NEG, s))
            top_first = jnp.maximum(top_first, jnp.where(e, s, NEG))
        top_late = jnp.max(top_late, axis=1, keepdims=True)
        top_first = jnp.max(top_first, axis=1, keepdims=True)
        p_late = [jnp.exp2((s - top_late) * coef) for s in late]
        p_first = jnp.exp2((first - top_first) * coef)
        p_chosen = [
            jnp.exp2((s - jnp.where(e, top_first, top_late)) * coef)
            for e, s in zip(early, chosen)
        ]
        sum_late = functools.reduce(jnp.add, p_late)
        sum_first = p_first
        for e, p in zip(early, p_chosen):
            sum_late = sum_late + jnp.where(e, 0.0, p)
            sum_first = sum_first + jnp.where(e, p, 0.0)
        sum_late = jnp.sum(sum_late, axis=1, keepdims=True)
        sum_first = jnp.sum(sum_first, axis=1, keepdims=True)

        def weighted(p, start, count):
            return jnp.dot(
                p.astype(jnp.bfloat16),
                val_s[pl.ds(start, count), cols],
                preferred_element_type=jnp.float32,
            )

        out_late = weighted(jnp.concatenate(p_late, 1), 0, (STEPS + 1) * HALF)
        out_first = weighted(p_first, 0, HALF)
        for j, e in enumerate(early):
            part = weighted(p_chosen[j], k_at[j], HALF)
            out_late = out_late + jnp.where(e, 0.0, part)
            out_first = out_first + jnp.where(e, part, 0.0)
        o_ref[:HALF, cols] = (out_first / sum_first).astype(jnp.bfloat16)
        o_ref[HALF:, cols] = (out_late / sum_late).astype(jnp.bfloat16)


def attend(first, heads, sel, lat, rot, q_nope, q_rot, weights, earlier):
    tok_len, all_cols = q_nope.shape
    width = 4
    cols = width * NOPE
    steps = heads // width
    count, depth = lat.shape

    def whole(shape):
        return pl.BlockSpec(shape, lambda i: (0, 0))

    def mine(shape):
        return pl.BlockSpec(shape, lambda i: (0, first // width + i))

    in_specs = [
        pl.BlockSpec(memory_space=pltpu.SMEM),
        whole(lat.shape),
        whole(rot.shape),
        mine((tok_len, cols)),
        mine((tok_len, cols)),
    ]
    in_specs.append(pl.BlockSpec(weights.shape[:2] + (cols,), lambda i: (0, 0, i)))
    in_specs.append(pl.BlockSpec(weights.shape[:2] + (cols,), lambda i: (0, 0, steps + i)))
    operands = [sel, lat, rot, q_nope, q_rot, weights, weights]
    aliases = {}
    if earlier is not None:
        in_specs.append(pl.BlockSpec(memory_space=pl.ANY))
        aliases = {len(operands): 0}
        operands.append(earlier)
    lane_cols = heads * NOPE
    flops = 4 * count * depth * lane_cols + heads * 7 * HALF * HALF * (2 * 256 + 2 * VDIM)
    return pl.pallas_call(
        functools.partial(attend_kernel, width),
        grid=(steps,),
        in_specs=in_specs,
        out_specs=mine((tok_len, cols)),
        out_shape=jax.ShapeDtypeStruct((tok_len, all_cols), jnp.bfloat16),
        scratch_shapes=[
            pltpu.VMEM((count, cols), jnp.bfloat16),
            pltpu.VMEM((count, cols), jnp.bfloat16),
        ],
        input_output_aliases=aliases,
        compiler_params=pltpu.CompilerParams(vmem_limit_bytes=40 * 1024 * 1024),
        cost_estimate=pl.CostEstimate(
            flops=flops,
            bytes_accessed=2 * (4 * depth * lane_cols + 3 * tok_len * lane_cols + count * 640),
            transcendentals=heads * 7 * HALF * HALF,
        ),
        name=f"attend_{first}",
    )(*operands)


def local(q_nope, q_rope, latent, k_rope, blocks, w_uk, w_uv):
    tok_len, all_cols = q_nope.shape
    quarter = latent.shape[0]
    w_rows = w_uk.shape[0]
    n_ctx = lax.axis_size("ctx")
    ctx_index = lax.axis_index("ctx")
    head_index = lax.axis_index("head")
    z, x = ctx_index // (NX * NY), (ctx_index // NY) % NX
    heads = all_cols // NOPE
    parts = [(0, 3 * heads // 4), (3 * heads // 4, heads // 4)]

    shard = jnp.concatenate(
        [w[:, f * NOPE : (f + n) * NOPE] for f, n in parts for w in (w_uk, w_uv)], 1
    )
    own_rows = gather_own(shard)

    own_pair = blocks[ctx_index]
    own_pos = shard_positions(own_pair, head_index * quarter, quarter, tok_len)
    own_rot = rotate(k_rope.astype(jnp.float32), angles_of(own_pos, ROPE)).astype(jnp.bfloat16)
    own = jnp.concatenate([latent, own_rot, own_rot], 1)
    visited = [own]
    for step in range(1, STEPS):
        pairs = [(source, (source + step) % n_ctx) for source in range(n_ctx)]
        visited.append(lax.ppermute(own, "ctx", pairs))
    held = jnp.stack(visited)
    across = lax.ppermute(held, "head", [(0, 2), (2, 0), (1, 3), (3, 1)])
    upper = head_index // 2 == 0
    two = jnp.stack([jnp.where(upper, held, across), jnp.where(upper, across, held)])
    both = lax.all_gather(two, "head", axis=0, axis_index_groups=[[0, 1], [2, 3]])
    both = both.transpose(1, 2, 0, 3, 4).reshape(STEPS * tok_len, own.shape[1])
    depth = latent.shape[1]
    lat_all, rot_all = both[:, :depth], both[:, depth:]

    order = row_order(plan_of(head_index), z, x, w_rows)
    place_of = lax.broadcasted_iota(jnp.int32, (depth, depth), 0) == order[None, :]
    lat_all = jnp.dot(lat_all, place_of.astype(jnp.bfloat16))

    query_pos = shard_positions(own_pair, 0, tok_len, tok_len)
    q_rot = rotate_queries(q_rope, angles_of(query_pos, ROPE))
    sel = jnp.stack(
        [
            (blocks[(ctx_index - step) % n_ctx, 0] < own_pair[0]).astype(jnp.int32)
            for step in range(1, STEPS)
        ]
    )
    zero = held[0, 0, 0] * 0 + held[1, 0, 0] * 0 + held[2, 0, 0] * 0 + q_rot[0, 0] * 0
    result = None
    for first, count in parts:
        cols = slice(2 * first * NOPE, 2 * (first + count) * NOPE)
        weights = gather_rest(own_rows[:, cols] + zero)
        result = attend(first, count, sel, lat_all, rot_all, q_nope, q_rot, weights, result)
    return result


def solution(mesh):
    in_specs = (
        P("ctx", "head"),
        P("ctx", "head"),
        P(("ctx", "head"), None),
        P(("ctx", "head"), None),
        P(),
        P("ctx", "head"),
        P("ctx", "head"),
    )
    out_specs = P("ctx", "head")
    return jax.shard_map(local, mesh=mesh, in_specs=in_specs, out_specs=out_specs, check_vma=False)
```

```python
import functools

import jax
import jax.numpy as jnp
from jax import lax
from jax.experimental import pallas as pl
from jax.experimental.pallas import tpu as pltpu
from jax.sharding import PartitionSpec as P

ROPE = 64
NOPE = 128
VDIM = 128
STEPS = 3
NZ, NX, NY = 8, 4, 4
N_HEAD = 4
HALF = 128
CHUNK = 32
LOG2E = 1.4426950408889634
NEG = -1e30


def place(z, x, y):
    return ((z % NZ) * NX + x % NX) * NY + y


def members(plan, colour):
    if plan == 0:
        return [(z, (colour - 2 * z) % NX) for z in range(NZ)]
    return [((colour - 2 * x) % 4 + 4 * far, x) for x in range(NX) for far in range(2)]


def plan_of(head):
    return head % 2


def colour_of(plan, z, x):
    return jnp.where(plan == 0, x + 2 * z, z + 2 * x) % 4


def gather_own(shard):
    groups = [
        [place(z, x, y) * N_HEAD + head for z, x in members(plan_of(head), c) for y in range(NY)]
        for head in range(N_HEAD)
        for c in range(4)
    ]
    size = len(groups[0])
    return lax.all_to_all(
        jnp.broadcast_to(shard[None], (size,) + shard.shape),
        ("ctx", "head"),
        0,
        0,
        axis_index_groups=groups,
    ).reshape(size * shard.shape[0], shard.shape[1])


def from_neighbour(value, step, along):
    pairs = []
    for head in range(N_HEAD):
        on_x = (plan_of(head) == 0) == (along == 0)
        dz, dx = (0, step) if on_x else (step, 0)
        pairs += [
            (place(z + dz, x + dx, y) * N_HEAD + head, place(z, x, y) * N_HEAD + head)
            for z in range(NZ)
            for x in range(NX)
            for y in range(NY)
        ]
    return lax.ppermute(value, ("ctx", "head"), pairs)


def gather_rest(own):
    mid = own.shape[0] // 2
    return (
        own,
        from_neighbour(own, 1, 0),
        from_neighbour(own, -1, 0),
        from_neighbour(own[:mid], 1, 1),
        from_neighbour(own[mid:], -1, 1),
    )


def row_order(plan, z, x, rows):
    at = jnp.arange(NZ * NX * NY * rows, dtype=jnp.int32)
    quarter = at.shape[0] // 4
    piece, rest = at // quarter, at % quarter
    step = jnp.where(piece < 2, piece, 5 - piece)
    colour = (colour_of(plan, z, x) + step) % 4
    member, inner = rest // (NY * rows), rest % (NY * rows)
    mz = jnp.where(plan == 0, member, (colour - 2 * (member // 2)) % 4 + 4 * (member % 2))
    mx = jnp.where(plan == 0, (colour - 2 * member) % 4, member // 2)
    return (mz * NX + mx) * (NY * rows) + inner


def angles_of(pos, width):
    half = width // 2
    freq = 10000.0 ** (-(2.0 * jnp.arange(half, dtype=jnp.float32)) / width)
    return pos.astype(jnp.float32)[..., None] * freq


def turned(x, cosine, sine):
    lane = lax.broadcasted_iota(jnp.int32, x.shape, 1)
    swapped = jnp.where(lane % 64 < 32, pltpu.roll(x, 96, 1), pltpu.roll(x, 32, 1))
    return x * cosine + swapped * sine


def rotate_queries_kernel(x_ref, cos_ref, sin_ref, o_ref):
    rows = x_ref.shape[0]
    left = lax.broadcasted_iota(jnp.int32, (rows, 128), 1) < 64

    def own(ref):
        return jnp.concatenate([ref[:HALF], ref[STEPS * HALF : (STEPS + 1) * HALF]], 0)

    cosine, sine = own(cos_ref), own(sin_ref)
    for pair in range(x_ref.shape[1] // 128):
        x = turned(x_ref[:, pair * 128 : (pair + 1) * 128].astype(jnp.float32), cosine, sine)
        high = x.astype(jnp.bfloat16).astype(jnp.float32)
        rest = x - high
        first = jnp.where(left, high, pltpu.roll(rest, 64, 1))
        second = jnp.where(left, pltpu.roll(high, 64, 1), rest)
        o_ref[:, pair * 256 : pair * 256 + 128] = first.astype(jnp.bfloat16)
        o_ref[:, pair * 256 + 128 : pair * 256 + 256] = second.astype(jnp.bfloat16)


def rotate_queries(q_rope, cosine, sine):
    tok_len, width = q_rope.shape
    return pl.pallas_call(
        rotate_queries_kernel,
        out_shape=jax.ShapeDtypeStruct((tok_len, 2 * width), jnp.bfloat16),
        cost_estimate=pl.CostEstimate(
            flops=4 * tok_len * width, bytes_accessed=6 * tok_len * width, transcendentals=0
        ),
        name="rotate_queries",
    )(q_rope, cosine, sine)


def prepare_keys_kernel(held_ref, order_ref, cos_ref, sin_ref, lat_ref, rot_ref):
    cores, halves, steps, _, _ = held_ref.shape
    depth = lat_ref.shape[1]
    held = jnp.concatenate(
        [
            held_ref[core, half, step]
            for half in range(halves)
            for step in range(steps)
            for core in range(cores)
        ],
        0,
    )
    at = lax.broadcasted_iota(jnp.int32, (depth, depth), 0)
    place_of = (at == order_ref[...]).astype(jnp.float32).astype(jnp.bfloat16)
    lat = jnp.dot(held[:, :depth], place_of, preferred_element_type=jnp.float32)
    lat_ref[...] = lat.astype(jnp.bfloat16)
    rot = turned(held[:, depth:].astype(jnp.float32), cos_ref[...], sin_ref[...])
    rot_ref[...] = rot.astype(jnp.bfloat16)


def prepare_keys(held, order, cosine, sine):
    depth = order.shape[0]
    count = cosine.shape[0]
    return pl.pallas_call(
        prepare_keys_kernel,
        out_shape=(
            jax.ShapeDtypeStruct((count, depth), jnp.bfloat16),
            jax.ShapeDtypeStruct((count, 128), jnp.bfloat16),
        ),
        cost_estimate=pl.CostEstimate(
            flops=2 * count * depth * depth, bytes_accessed=6 * count * 640, transcendentals=0
        ),
        compiler_params=pltpu.CompilerParams(vmem_limit_bytes=32 * 1024 * 1024),
        name="prepare_keys",
    )(held, order[None, :], cosine, sine)


def attend_kernel(width, sel_ref, lat_ref, rot_ref, qn_ref, qr_ref, *refs):
    o_ref, key_s, val_s, score_s, prob_s, sum_s = refs[-6:]
    lat = lat_ref[...]
    pieces = (len(refs) - 6) // 2
    up_k = jnp.concatenate([r[...] for r in refs[:pieces]], 0)
    up_v = jnp.concatenate([r[...] for r in refs[pieces : 2 * pieces]], 0)
    key_s[...] = jnp.dot(lat, up_k, preferred_element_type=jnp.float32).astype(jnp.bfloat16)
    val_s[...] = jnp.dot(lat, up_v, preferred_element_type=jnp.float32).astype(jnp.bfloat16)
    coef = LOG2E / (NOPE + ROPE) ** 0.5
    contract = (((1,), (1,)), ((), ()))
    early = [sel_ref[j] != 0 for j in range(STEPS - 1)]
    q_at = [pl.multiple_of(jnp.where(e, 0, HALF), HALF) for e in early]
    k_at = [
        pl.multiple_of(jnp.where(e, j + 1, STEPS + j + 1) * HALF, HALF)
        for j, e in enumerate(early)
    ]
    full = (STEPS + 1) * HALF
    chosen_at = [full + (j + 1) * HALF for j in range(STEPS - 1)]

    for h in range(width):
        cols = slice(h * NOPE, (h + 1) * NOPE)

        def scores(at, q_start, k_start, count):
            q_rows, k_rows = pl.ds(q_start, HALF), pl.ds(k_start, count)
            q = jnp.concatenate([qn_ref[q_rows, cols], qr_ref[q_rows, cols]], 1)
            k = jnp.concatenate([key_s[k_rows, cols], rot_ref[k_rows, :]], 1)
            score_s[h, :, at : at + count] = lax.dot_general(
                q, k, contract, preferred_element_type=jnp.float32
            )

        scores(0, HALF, 0, full)
        scores(full, 0, 0, HALF)
        for j in range(STEPS - 1):
            scores(chosen_at[j], q_at[j], k_at[j], HALF)

    for h in range(width):
        cols = slice(h * NOPE, (h + 1) * NOPE)
        for start in range(0, HALF, CHUNK):
            rows = slice(start, start + CHUNK)
            row = lax.broadcasted_iota(jnp.int32, (CHUNK, HALF), 0) + start
            causal = lax.broadcasted_iota(jnp.int32, (CHUNK, HALF), 1) <= row
            late = [score_s[h, rows, i * HALF : (i + 1) * HALF] for i in range(STEPS + 1)]
            late[STEPS] = jnp.where(causal, late[STEPS], NEG)
            first = jnp.where(causal, score_s[h, rows, full : full + HALF], NEG)
            chosen = [score_s[h, rows, at : at + HALF] for at in chosen_at]
            top_late = functools.reduce(jnp.maximum, late)
            top_first = first
            for e, s in zip(early, chosen):
                top_late = jnp.maximum(top_late, jnp.where(e, NEG, s))
                top_first = jnp.maximum(top_first, jnp.where(e, s, NEG))
            top_late = jnp.max(top_late, axis=1, keepdims=True)
            top_first = jnp.max(top_first, axis=1, keepdims=True)
            sum_late = jnp.zeros((CHUNK, HALF), jnp.float32)
            for i, s in enumerate(late):
                p = jnp.exp2((s - top_late) * coef)
                sum_late = sum_late + p
                prob_s[h, rows, i * HALF : (i + 1) * HALF] = p.astype(jnp.bfloat16)
            p = jnp.exp2((first - top_first) * coef)
            sum_first = p
            prob_s[h, rows, full : full + HALF] = p.astype(jnp.bfloat16)
            for e, s, at in zip(early, chosen, chosen_at):
                p = jnp.exp2((s - jnp.where(e, top_first, top_late)) * coef)
                sum_late = sum_late + jnp.where(e, 0.0, p)
                sum_first = sum_first + jnp.where(e, p, 0.0)
                prob_s[h, rows, at : at + HALF] = p.astype(jnp.bfloat16)
            sum_s[h, 0, rows, :] = jnp.sum(sum_late, axis=1, keepdims=True)
            sum_s[h, 1, rows, :] = jnp.sum(sum_first, axis=1, keepdims=True)

        def weighted(at, k_start, count):
            return jnp.dot(
                prob_s[h, :, at : at + count],
                val_s[pl.ds(k_start, count), cols],
                preferred_element_type=jnp.float32,
            )

        out_late = weighted(0, 0, full)
        out_first = weighted(full, 0, HALF)
        for j, e in enumerate(early):
            part = weighted(chosen_at[j], k_at[j], HALF)
            out_late = out_late + jnp.where(e, 0.0, part)
            out_first = out_first + jnp.where(e, part, 0.0)
        o_ref[:HALF, cols] = (out_first / sum_s[h, 1]).astype(jnp.bfloat16)
        o_ref[HALF:, cols] = (out_late / sum_s[h, 0]).astype(jnp.bfloat16)


def attend(sel, lat, rot, q_nope, q_rot, weights):
    tok_len, all_cols = q_nope.shape
    width = 4
    cols = width * NOPE
    heads = all_cols // NOPE
    steps = heads // width
    count, depth = lat.shape
    blocks = 2 * STEPS + 1

    def whole(shape):
        return pl.BlockSpec(shape, lambda i: (0, 0))

    def mine(shape):
        return pl.BlockSpec(shape, lambda i: (0, i))

    in_specs = [
        pl.BlockSpec(memory_space=pltpu.SMEM),
        whole(lat.shape),
        whole(rot.shape),
        mine((tok_len, cols)),
        mine((tok_len, cols)),
    ]
    in_specs += [pl.BlockSpec((w.shape[0], cols), lambda i: (0, i)) for w in weights]
    in_specs += [pl.BlockSpec((w.shape[0], cols), lambda i: (0, steps + i)) for w in weights]
    flops = 4 * count * depth * all_cols + heads * blocks * HALF * HALF * (2 * 256 + 2 * VDIM)
    return pl.pallas_call(
        functools.partial(attend_kernel, width),
        grid=(steps,),
        in_specs=in_specs,
        out_specs=mine((tok_len, cols)),
        out_shape=jax.ShapeDtypeStruct((tok_len, all_cols), jnp.bfloat16),
        scratch_shapes=[
            pltpu.VMEM((count, cols), jnp.bfloat16),
            pltpu.VMEM((count, cols), jnp.bfloat16),
            pltpu.VMEM((width, HALF, blocks * HALF), jnp.float32),
            pltpu.VMEM((width, HALF, blocks * HALF), jnp.bfloat16),
            pltpu.VMEM((width, 2, HALF, 1), jnp.float32),
        ],
        compiler_params=pltpu.CompilerParams(vmem_limit_bytes=40 * 1024 * 1024),
        cost_estimate=pl.CostEstimate(
            flops=flops,
            bytes_accessed=2 * (4 * depth * all_cols + 3 * tok_len * all_cols + count * 640),
            transcendentals=heads * blocks * HALF * HALF,
        ),
        name="attend",
    )(sel, lat, rot, q_nope, q_rot, *weights, *weights)


def local(q_nope, q_rope, latent, k_rope, blocks, w_uk, w_uv):
    w_rows = w_uk.shape[0]
    n_ctx = lax.axis_size("ctx")
    ctx_index = lax.axis_index("ctx")
    head_index = lax.axis_index("head")
    z, x = ctx_index // (NX * NY), (ctx_index // NY) % NX
    own = jnp.concatenate([latent, k_rope, k_rope], 1)
    visited = [own]
    for step in range(1, STEPS):
        pairs = [(source, (source + step) % n_ctx) for source in range(n_ctx)]
        visited.append(lax.ppermute(own, "ctx", pairs))
    held = jnp.stack(visited)

    own_rows = gather_own(jnp.concatenate([w_uk, w_uv], 1))

    shards = [(ctx_index - step) % n_ctx for step in range(STEPS)]
    rows = jnp.arange(HALF, dtype=jnp.int32)
    pos = jnp.concatenate([blocks[c, half] * HALF + rows for half in range(2) for c in shards])
    angles = angles_of(pos, ROPE)
    cosine, sine = jnp.cos(angles), jnp.sin(angles)
    cosine = jnp.concatenate([cosine] * 4, 1)
    sine = jnp.concatenate([-sine, sine, -sine, sine], 1)
    q_rot = rotate_queries(q_rope, cosine, sine)
    sel = jnp.stack([(blocks[c, 0] < blocks[ctx_index, 0]).astype(jnp.int32) for c in shards[1:]])

    zero = held[0, 0, 0] * 0 + held[1, 0, 0] * 0 + held[2, 0, 0] * 0 + q_rot[0, 0] * 0
    weights = gather_rest(own_rows + zero)

    across = lax.ppermute(held, "head", [(0, 2), (2, 0), (1, 3), (3, 1)])
    upper = head_index // 2 == 0
    two = jnp.stack([jnp.where(upper, held, across), jnp.where(upper, across, held)])
    both = lax.all_gather(two, "head", axis=0, axis_index_groups=[[0, 1], [2, 3]])
    order = row_order(plan_of(head_index), z, x, w_rows)
    lat, rot = prepare_keys(both, order, cosine, sine)
    return attend(sel, lat, rot, q_nope, q_rot, weights)


def solution(mesh):
    in_specs = (
        P("ctx", "head"),
        P("ctx", "head"),
        P(("ctx", "head"), None),
        P(("ctx", "head"), None),
        P(),
        P("ctx", "head"),
        P("ctx", "head"),
    )
    out_specs = P("ctx", "head")
    return jax.shard_map(local, mesh=mesh, in_specs=in_specs, out_specs=out_specs, check_vma=False)
```

```python
import functools

import jax
import jax.numpy as jnp
from jax import lax
from jax.experimental import pallas as pl
from jax.experimental.pallas import tpu as pltpu
from jax.sharding import PartitionSpec as P

ROPE = 64
NOPE = 128
VDIM = 128
STEPS = 3
NZ, NX, NY = 8, 4, 4
N_HEAD = 4
HALF = 128
CHUNK = 32
LOG2E = 1.4426950408889634
NEG = -1e30


def place(z, x, y):
    return ((z % NZ) * NX + x % NX) * NY + y


def members(plan, colour):
    if plan == 0:
        return [(z, (colour - 2 * z) % NX) for z in range(NZ)]
    return [((colour - 2 * x) % 4 + 4 * far, x) for x in range(NX) for far in range(2)]


def plan_of(head):
    return head % 2


def colour_of(plan, z, x):
    return jnp.where(plan == 0, x + 2 * z, z + 2 * x) % 4


def spread(value, groups):
    size = len(groups[0])
    return lax.all_to_all(
        jnp.broadcast_to(value[None], (size,) + value.shape),
        ("ctx", "head"),
        0,
        0,
        axis_index_groups=groups,
    ).reshape(size * value.shape[0], value.shape[1])


def gather_own(shard):
    lines = [
        [place(z, x, y) * N_HEAD + head for y in range(NY)]
        for head in range(N_HEAD)
        for z in range(NZ)
        for x in range(NX)
    ]
    colours = [
        [place(z, x, y) * N_HEAD + head for z, x in members(plan_of(head), c)]
        for head in range(N_HEAD)
        for c in range(4)
        for y in range(NY)
    ]
    return spread(spread(shard, lines), colours)


def from_neighbour(value, step, along):
    pairs = []
    for head in range(N_HEAD):
        on_x = (plan_of(head) == 0) == (along == 0)
        dz, dx = (0, step) if on_x else (step, 0)
        pairs += [
            (place(z + dz, x + dx, y) * N_HEAD + head, place(z, x, y) * N_HEAD + head)
            for z in range(NZ)
            for x in range(NX)
            for y in range(NY)
        ]
    return lax.ppermute(value, ("ctx", "head"), pairs)


def gather_rest(own, side):
    return own, from_neighbour(own, 1, 0), from_neighbour(own, -1, 0), from_neighbour(own, side, 1)


def row_order(plan, z, x, rows):
    at = jnp.arange(NZ * NX * NY * rows, dtype=jnp.int32)
    quarter = at.shape[0] // 4
    piece, rest = at // quarter, at % quarter
    step = jnp.where(piece < 2, piece, 5 - piece)
    colour = (colour_of(plan, z, x) + step) % 4
    member, inner = rest // (NY * rows), rest % (NY * rows)
    mz = jnp.where(plan == 0, member, (colour - 2 * (member // 2)) % 4 + 4 * (member % 2))
    mx = jnp.where(plan == 0, (colour - 2 * member) % 4, member // 2)
    return (mz * NX + mx) * (NY * rows) + inner


def factors(cosine, sine):
    return (
        jnp.concatenate([cosine] * 4, 0).T,
        jnp.concatenate([-sine, sine, -sine, sine], 0).T,
    )


def turned(x, cosine, sine):
    lane = lax.broadcasted_iota(jnp.int32, x.shape, 1)
    swapped = jnp.where(lane % 64 < 32, pltpu.roll(x, 96, 1), pltpu.roll(x, 32, 1))
    return x * cosine + swapped * sine


def rotate_queries_kernel(x_ref, cos_ref, sin_ref, o_ref, cos_s, sin_s):
    rows = x_ref.shape[0]
    left = lax.broadcasted_iota(jnp.int32, (rows, 128), 1) < 64

    @pl.when(pl.program_id(0) == 0)
    def _():
        def own(ref):
            late = STEPS * HALF
            return jnp.concatenate([ref[:, :HALF], ref[:, late : late + HALF]], 1)

        cos_s[...], sin_s[...] = factors(own(cos_ref), own(sin_ref))

    cosine, sine = cos_s[...], sin_s[...]
    for pair in range(x_ref.shape[1] // 128):
        x = turned(x_ref[:, pair * 128 : (pair + 1) * 128].astype(jnp.float32), cosine, sine)
        high = x.astype(jnp.bfloat16).astype(jnp.float32)
        rest = x - high
        first = jnp.where(left, high, pltpu.roll(rest, 64, 1))
        second = jnp.where(left, pltpu.roll(high, 64, 1), rest)
        o_ref[:, pair * 256 : pair * 256 + 128] = first.astype(jnp.bfloat16)
        o_ref[:, pair * 256 + 128 : pair * 256 + 256] = second.astype(jnp.bfloat16)


def rotate_queries(q_rope, cosine, sine):
    tok_len, width = q_rope.shape
    return pl.pallas_call(
        rotate_queries_kernel,
        grid=(4,),
        in_specs=[
            pl.BlockSpec((tok_len, width // 4), lambda i: (0, i)),
            pl.BlockSpec(cosine.shape, lambda i: (0, 0)),
            pl.BlockSpec(sine.shape, lambda i: (0, 0)),
        ],
        out_specs=pl.BlockSpec((tok_len, width // 2), lambda i: (0, i)),
        out_shape=jax.ShapeDtypeStruct((tok_len, 2 * width), jnp.bfloat16),
        scratch_shapes=[pltpu.VMEM((tok_len, 128), jnp.float32)] * 2,
        cost_estimate=pl.CostEstimate(
            flops=4 * tok_len * width, bytes_accessed=6 * tok_len * width, transcendentals=0
        ),
        name="rotate_queries",
    )(q_rope, cosine, sine)


def prepare_keys_kernel(held_ref, order_ref, cos_ref, sin_ref, lat_ref, rot_ref):
    cores, halves, steps, _, _ = held_ref.shape
    depth = lat_ref.shape[1]
    held = jnp.concatenate(
        [
            held_ref[core, half, step]
            for half in range(halves)
            for step in range(steps)
            for core in range(cores)
        ],
        0,
    )
    at = lax.broadcasted_iota(jnp.int32, (depth, depth), 0)
    place_of = (at == order_ref[...]).astype(jnp.float32).astype(jnp.bfloat16)
    lat = jnp.dot(held[:, :depth], place_of, preferred_element_type=jnp.float32)
    lat_ref[...] = lat.astype(jnp.bfloat16)
    rot = turned(held[:, depth:].astype(jnp.float32), *factors(cos_ref[...], sin_ref[...]))
    rot_ref[...] = rot.astype(jnp.bfloat16)


def prepare_keys(held, order, cosine, sine):
    depth = order.shape[0]
    count = cosine.shape[1]
    return pl.pallas_call(
        prepare_keys_kernel,
        out_shape=(
            jax.ShapeDtypeStruct((count, depth), jnp.bfloat16),
            jax.ShapeDtypeStruct((count, 128), jnp.bfloat16),
        ),
        cost_estimate=pl.CostEstimate(
            flops=2 * count * depth * depth, bytes_accessed=6 * count * 640, transcendentals=0
        ),
        compiler_params=pltpu.CompilerParams(vmem_limit_bytes=32 * 1024 * 1024),
        name="prepare_keys",
    )(held, order[None, :], cosine, sine)


def attend_kernel(width, sel_ref, lat_ref, rot_ref, qn_ref, qr_ref, *refs):
    o_ref, key_s, val_s, score_s, prob_s, sum_s = refs[-6:]
    lat = lat_ref[...]
    pieces = 4
    up_k = jnp.concatenate([r[...] for r in refs[:pieces]], 0)
    up_v = jnp.concatenate([r[...] for r in refs[pieces : 2 * pieces]], 0)
    key_s[...] = jnp.dot(lat, up_k, preferred_element_type=jnp.float32).astype(jnp.bfloat16)
    val_s[...] = jnp.dot(lat, up_v, preferred_element_type=jnp.float32).astype(jnp.bfloat16)
    coef = LOG2E / (NOPE + ROPE) ** 0.5
    contract = (((1,), (1,)), ((), ()))
    early = [sel_ref[j] != 0 for j in range(STEPS - 1)]
    q_at = [pl.multiple_of(jnp.where(e, 0, HALF), HALF) for e in early]
    k_at = [
        pl.multiple_of(jnp.where(e, j + 1, STEPS + j + 1) * HALF, HALF)
        for j, e in enumerate(early)
    ]
    full = (STEPS + 1) * HALF
    chosen_at = [full + (j + 1) * HALF for j in range(STEPS - 1)]

    for h in range(width):
        cols = slice(h * NOPE, (h + 1) * NOPE)

        def scores(at, q_start, k_start, count):
            q_rows, k_rows = pl.ds(q_start, HALF), pl.ds(k_start, count)
            q = jnp.concatenate([qn_ref[q_rows, cols], qr_ref[q_rows, cols]], 1)
            k = jnp.concatenate([key_s[k_rows, cols], rot_ref[k_rows, :]], 1)
            score_s[h, :, at : at + count] = lax.dot_general(
                q, k, contract, preferred_element_type=jnp.float32
            )

        scores(0, HALF, 0, full)
        scores(full, 0, 0, HALF)
        for j in range(STEPS - 1):
            scores(chosen_at[j], q_at[j], k_at[j], HALF)

    for h in range(width):
        cols = slice(h * NOPE, (h + 1) * NOPE)
        for start in range(0, HALF, CHUNK):
            rows = slice(start, start + CHUNK)
            row = lax.broadcasted_iota(jnp.int32, (CHUNK, HALF), 0) + start
            causal = lax.broadcasted_iota(jnp.int32, (CHUNK, HALF), 1) <= row
            late = [score_s[h, rows, i * HALF : (i + 1) * HALF] for i in range(STEPS + 1)]
            late[STEPS] = jnp.where(causal, late[STEPS], NEG)
            first = jnp.where(causal, score_s[h, rows, full : full + HALF], NEG)
            chosen = [score_s[h, rows, at : at + HALF] for at in chosen_at]
            top_late = functools.reduce(jnp.maximum, late)
            top_first = first
            for e, s in zip(early, chosen):
                top_late = jnp.maximum(top_late, jnp.where(e, NEG, s))
                top_first = jnp.maximum(top_first, jnp.where(e, s, NEG))
            top_late = jnp.max(top_late, axis=1, keepdims=True)
            top_first = jnp.max(top_first, axis=1, keepdims=True)
            sum_late = jnp.zeros((CHUNK, HALF), jnp.float32)
            for i, s in enumerate(late):
                p = jnp.exp2((s - top_late) * coef)
                sum_late = sum_late + p
                prob_s[h, rows, i * HALF : (i + 1) * HALF] = p.astype(jnp.bfloat16)
            p = jnp.exp2((first - top_first) * coef)
            sum_first = p
            prob_s[h, rows, full : full + HALF] = p.astype(jnp.bfloat16)
            for e, s, at in zip(early, chosen, chosen_at):
                p = jnp.exp2((s - jnp.where(e, top_first, top_late)) * coef)
                sum_late = sum_late + jnp.where(e, 0.0, p)
                sum_first = sum_first + jnp.where(e, p, 0.0)
                prob_s[h, rows, at : at + HALF] = p.astype(jnp.bfloat16)
            sum_s[h, 0, rows, :] = jnp.sum(sum_late, axis=1, keepdims=True)
            sum_s[h, 1, rows, :] = jnp.sum(sum_first, axis=1, keepdims=True)

        def weighted(at, k_start, count):
            return jnp.dot(
                prob_s[h, :, at : at + count],
                val_s[pl.ds(k_start, count), cols],
                preferred_element_type=jnp.float32,
            )

        out_late = weighted(0, 0, full)
        out_first = weighted(full, 0, HALF)
        for j, e in enumerate(early):
            part = weighted(chosen_at[j], k_at[j], HALF)
            out_late = out_late + jnp.where(e, 0.0, part)
            out_first = out_first + jnp.where(e, part, 0.0)
        o_ref[:HALF, cols] = (out_first / sum_s[h, 1]).astype(jnp.bfloat16)
        o_ref[HALF:, cols] = (out_late / sum_s[h, 0]).astype(jnp.bfloat16)


def attend(first, heads, sel, lat, rot, q_nope, q_rot, weights, earlier):
    tok_len, all_cols = q_nope.shape
    width = 4
    cols = width * NOPE
    steps = heads // width
    count, depth = lat.shape
    blocks = 2 * STEPS + 1

    def whole(shape):
        return pl.BlockSpec(shape, lambda i: (0, 0))

    def mine(shape):
        return pl.BlockSpec(shape, lambda i: (0, first // width + i))

    in_specs = [
        pl.BlockSpec(memory_space=pltpu.SMEM),
        whole(lat.shape),
        whole(rot.shape),
        mine((tok_len, cols)),
        mine((tok_len, cols)),
    ]
    in_specs += [pl.BlockSpec((w.shape[0], cols), lambda i: (0, i)) for w in weights]
    in_specs += [pl.BlockSpec((w.shape[0], cols), lambda i: (0, steps + i)) for w in weights]
    operands = [sel, lat, rot, q_nope, q_rot, *weights, *weights]
    aliases = {}
    if earlier is not None:
        in_specs.append(pl.BlockSpec(memory_space=pl.ANY))
        aliases = {len(operands): 0}
        operands.append(earlier)
    some = heads * NOPE
    flops = 4 * count * depth * some + heads * blocks * HALF * HALF * (2 * 256 + 2 * VDIM)
    return pl.pallas_call(
        functools.partial(attend_kernel, width),
        grid=(steps,),
        in_specs=in_specs,
        out_specs=mine((tok_len, cols)),
        out_shape=jax.ShapeDtypeStruct((tok_len, all_cols), jnp.bfloat16),
        scratch_shapes=[
            pltpu.VMEM((count, cols), jnp.bfloat16),
            pltpu.VMEM((count, cols), jnp.bfloat16),
            pltpu.VMEM((width, HALF, blocks * HALF), jnp.float32),
            pltpu.VMEM((width, HALF, blocks * HALF), jnp.bfloat16),
            pltpu.VMEM((width, 2, HALF, 1), jnp.float32),
        ],
        input_output_aliases=aliases,
        compiler_params=pltpu.CompilerParams(vmem_limit_bytes=40 * 1024 * 1024),
        cost_estimate=pl.CostEstimate(
            flops=flops,
            bytes_accessed=2 * (4 * depth * some + 3 * tok_len * some + count * 640),
            transcendentals=heads * blocks * HALF * HALF,
        ),
        name=f"attend_{first}",
    )(*operands)


def local(q_nope, q_rope, latent, k_rope, blocks, w_uk, w_uv):
    w_rows = w_uk.shape[0]
    parts = [(0, 12), (12, 4)]
    n_ctx = lax.axis_size("ctx")
    ctx_index = lax.axis_index("ctx")
    head_index = lax.axis_index("head")
    z, x = ctx_index // (NX * NY), (ctx_index // NY) % NX
    own = jnp.concatenate([latent, k_rope, k_rope], 1)
    visited = [own]
    for step in range(1, STEPS):
        pairs = [(source, (source + step) % n_ctx) for source in range(n_ctx)]
        visited.append(lax.ppermute(own, "ctx", pairs))
    held = jnp.stack(visited)

    own_rows = gather_own(
        jnp.concatenate([w[:, f * NOPE : (f + n) * NOPE] for f, n in parts for w in (w_uk, w_uv)], 1)
    )

    shards = (ctx_index - jnp.arange(STEPS, dtype=jnp.int32)) % n_ctx
    at = jnp.arange(n_ctx, dtype=jnp.int32)[:, None] == shards[None, :]
    pairs_of = jnp.sum(jnp.where(at[:, None, :], blocks[:, :, None], 0), axis=0)
    rows = jnp.arange(HALF, dtype=jnp.int32)
    pos = (pairs_of[:, :, None] * HALF + rows).reshape(-1)
    half = ROPE // 2
    freq = 10000.0 ** (-(2.0 * jnp.arange(half, dtype=jnp.float32)) / ROPE)
    angles = pos.astype(jnp.float32)[None, :] * freq[:, None]
    cosine, sine = jnp.cos(angles), jnp.sin(angles)
    q_rot = rotate_queries(q_rope, cosine, sine)
    sel = (pairs_of[0, 1:] < pairs_of[0, 0]).astype(jnp.int32)

    across = lax.ppermute(held, "head", [(0, 2), (2, 0), (1, 3), (3, 1)])
    upper = head_index // 2 == 0
    weights = []
    for i, (first, count) in enumerate(parts):
        cols = slice(2 * first * NOPE, 2 * (first + count) * NOPE)
        some = own_rows[:, cols] if i else lax.optimization_barrier(own_rows)[:, cols] + q_rot[0, 0] * 0
        weights.append(gather_rest(some, 1 - 2 * i))
    two = jnp.stack([jnp.where(upper, held, across), jnp.where(upper, across, held)])
    both = lax.all_gather(two, "head", axis=0, axis_index_groups=[[0, 1], [2, 3]])
    order = row_order(plan_of(head_index), z, x, w_rows)
    lat, rot = prepare_keys(both, order, cosine, sine)
    result = None
    for (first, count), some in zip(parts, weights):
        result = attend(first, count, sel, lat, rot, q_nope, q_rot, some, result)
    return result


def solution(mesh):
    in_specs = (
        P("ctx", "head"),
        P("ctx", "head"),
        P(("ctx", "head"), None),
        P(("ctx", "head"), None),
        P(),
        P("ctx", "head"),
        P("ctx", "head"),
    )
    out_specs = P("ctx", "head")
    return jax.shard_map(local, mesh=mesh, in_specs=in_specs, out_specs=out_specs, check_vma=False)
```

```python
import functools

import jax
import jax.numpy as jnp
from jax import lax
from jax.experimental import pallas as pl
from jax.experimental.pallas import tpu as pltpu
from jax.sharding import PartitionSpec as P

ROPE = 64
NOPE = 128
VDIM = 128
STEPS = 3
NZ, NX, NY = 8, 4, 4
N_HEAD = 4
HALF = 128
CHUNK = 32
LOG2E = 1.4426950408889634
NEG = -1e30


def place(z, x, y):
    return ((z % NZ) * NX + x % NX) * NY + y


def members(plan, colour):
    if plan == 0:
        return [(z, (colour - 2 * z) % NX) for z in range(NZ)]
    return [((colour - 2 * x) % 4 + 4 * far, x) for x in range(NX) for far in range(2)]


def plan_of(head):
    return head % 2


def colour_of(plan, z, x):
    return jnp.where(plan == 0, x + 2 * z, z + 2 * x) % 4


def spread(value, groups):
    size = len(groups[0])
    return lax.all_to_all(
        jnp.broadcast_to(value[None], (size,) + value.shape),
        ("ctx", "head"),
        0,
        0,
        axis_index_groups=groups,
    ).reshape(size * value.shape[0], value.shape[1])


def gather_own(shard):
    lines = [
        [place(z, x, y) * N_HEAD + head for y in range(NY)]
        for head in range(N_HEAD)
        for z in range(NZ)
        for x in range(NX)
    ]
    colours = [
        [place(z, x, y) * N_HEAD + head for z, x in members(plan_of(head), c)]
        for head in range(N_HEAD)
        for c in range(4)
        for y in range(NY)
    ]
    return spread(spread(shard, lines), colours)


def from_neighbour(value, step, along):
    pairs = []
    for head in range(N_HEAD):
        on_x = (plan_of(head) == 0) == (along == 0)
        dz, dx = (0, step) if on_x else (step, 0)
        pairs += [
            (place(z + dz, x + dx, y) * N_HEAD + head, place(z, x, y) * N_HEAD + head)
            for z in range(NZ)
            for x in range(NX)
            for y in range(NY)
        ]
    return lax.ppermute(value, ("ctx", "head"), pairs)


def gather_rest(own, side):
    return own, from_neighbour(own, 1, 0), from_neighbour(own, -1, 0), from_neighbour(own, side, 1)


def row_order(plan, z, x, rows):
    at = jnp.arange(NZ * NX * NY * rows, dtype=jnp.int32)
    quarter = at.shape[0] // 4
    piece, rest = at // quarter, at % quarter
    step = jnp.where(piece < 2, piece, 5 - piece)
    colour = (colour_of(plan, z, x) + step) % 4
    member, inner = rest // (NY * rows), rest % (NY * rows)
    mz = jnp.where(plan == 0, member, (colour - 2 * (member // 2)) % 4 + 4 * (member % 2))
    mx = jnp.where(plan == 0, (colour - 2 * member) % 4, member // 2)
    return (mz * NX + mx) * (NY * rows) + inner


def factors(cosine, sine):
    return (
        jnp.concatenate([cosine] * 4, 0).T,
        jnp.concatenate([-sine, sine, -sine, sine], 0).T,
    )


def turned(x, cosine, sine):
    lane = lax.broadcasted_iota(jnp.int32, x.shape, 1)
    swapped = jnp.where(lane % 64 < 32, pltpu.roll(x, 96, 1), pltpu.roll(x, 32, 1))
    return x * cosine + swapped * sine


def rotate_queries_kernel(x_ref, cos_ref, sin_ref, o_ref, cos_s, sin_s):
    rows = x_ref.shape[0]
    left = lax.broadcasted_iota(jnp.int32, (rows, 128), 1) < 64

    @pl.when(pl.program_id(0) == 0)
    def _():
        def own(ref):
            late = STEPS * HALF
            return jnp.concatenate([ref[:, :HALF], ref[:, late : late + HALF]], 1)

        cos_s[...], sin_s[...] = factors(own(cos_ref), own(sin_ref))

    cosine, sine = cos_s[...], sin_s[...]
    for pair in range(x_ref.shape[1] // 128):
        x = turned(x_ref[:, pair * 128 : (pair + 1) * 128].astype(jnp.float32), cosine, sine)
        high = x.astype(jnp.bfloat16).astype(jnp.float32)
        rest = x - high
        first = jnp.where(left, high, pltpu.roll(rest, 64, 1))
        second = jnp.where(left, pltpu.roll(high, 64, 1), rest)
        o_ref[:, pair * 256 : pair * 256 + 128] = first.astype(jnp.bfloat16)
        o_ref[:, pair * 256 + 128 : pair * 256 + 256] = second.astype(jnp.bfloat16)


def rotate_queries(q_rope, cosine, sine):
    tok_len, width = q_rope.shape
    return pl.pallas_call(
        rotate_queries_kernel,
        grid=(4,),
        in_specs=[
            pl.BlockSpec((tok_len, width // 4), lambda i: (0, i)),
            pl.BlockSpec(cosine.shape, lambda i: (0, 0)),
            pl.BlockSpec(sine.shape, lambda i: (0, 0)),
        ],
        out_specs=pl.BlockSpec((tok_len, width // 2), lambda i: (0, i)),
        out_shape=jax.ShapeDtypeStruct((tok_len, 2 * width), jnp.bfloat16),
        scratch_shapes=[pltpu.VMEM((tok_len, 128), jnp.float32)] * 2,
        cost_estimate=pl.CostEstimate(
            flops=4 * tok_len * width, bytes_accessed=6 * tok_len * width, transcendentals=0
        ),
        name="rotate_queries",
    )(q_rope, cosine, sine)


def prepare_keys_kernel(held_ref, order_ref, cos_ref, sin_ref, lat_ref, rot_ref):
    cores, halves, steps, _, _ = held_ref.shape
    depth = lat_ref.shape[1]
    held = jnp.concatenate(
        [
            held_ref[core, half, step]
            for half in range(halves)
            for step in range(steps)
            for core in range(cores)
        ],
        0,
    )
    at = lax.broadcasted_iota(jnp.int32, (depth, depth), 0)
    place_of = (at == order_ref[...]).astype(jnp.float32).astype(jnp.bfloat16)
    lat = jnp.dot(held[:, :depth], place_of, preferred_element_type=jnp.float32)
    lat_ref[...] = lat.astype(jnp.bfloat16)
    rot = turned(held[:, depth:].astype(jnp.float32), *factors(cos_ref[...], sin_ref[...]))
    rot_ref[...] = rot.astype(jnp.bfloat16)


def prepare_keys(held, order, cosine, sine):
    depth = order.shape[0]
    count = cosine.shape[1]
    return pl.pallas_call(
        prepare_keys_kernel,
        out_shape=(
            jax.ShapeDtypeStruct((count, depth), jnp.bfloat16),
            jax.ShapeDtypeStruct((count, 128), jnp.bfloat16),
        ),
        cost_estimate=pl.CostEstimate(
            flops=2 * count * depth * depth, bytes_accessed=6 * count * 640, transcendentals=0
        ),
        compiler_params=pltpu.CompilerParams(vmem_limit_bytes=32 * 1024 * 1024),
        name="prepare_keys",
    )(held, order[None, :], cosine, sine)


def attend_kernel(width, sel_ref, lat_ref, rot_ref, qn_ref, qr_ref, *refs):
    o_ref, key_s, val_s, score_s, prob_s, sum_s = refs[-6:]
    lat = lat_ref[...]
    pieces = 4
    up_k = jnp.concatenate([r[...] for r in refs[:pieces]], 0)
    up_v = jnp.concatenate([r[...] for r in refs[pieces : 2 * pieces]], 0)
    key_s[...] = jnp.dot(lat, up_k, preferred_element_type=jnp.float32).astype(jnp.bfloat16)
    val_s[...] = jnp.dot(lat, up_v, preferred_element_type=jnp.float32).astype(jnp.bfloat16)
    coef = LOG2E / (NOPE + ROPE) ** 0.5
    contract = (((1,), (1,)), ((), ()))
    early = [sel_ref[j] != 0 for j in range(STEPS - 1)]
    q_at = [pl.multiple_of(jnp.where(e, 0, HALF), HALF) for e in early]
    k_at = [
        pl.multiple_of(jnp.where(e, j + 1, STEPS + j + 1) * HALF, HALF)
        for j, e in enumerate(early)
    ]
    full = (STEPS + 1) * HALF
    chosen_at = [full + (j + 1) * HALF for j in range(STEPS - 1)]

    for h in range(width):
        cols = slice(h * NOPE, (h + 1) * NOPE)

        def scores(at, q_start, k_start, count):
            q_rows, k_rows = pl.ds(q_start, HALF), pl.ds(k_start, count)
            q = jnp.concatenate([qn_ref[q_rows, cols], qr_ref[q_rows, cols]], 1)
            k = jnp.concatenate([key_s[k_rows, cols], rot_ref[k_rows, :]], 1)
            score_s[h, :, at : at + count] = lax.dot_general(
                q, k, contract, preferred_element_type=jnp.float32
            )

        scores(0, HALF, 0, full)
        scores(full, 0, 0, HALF)
        for j in range(STEPS - 1):
            scores(chosen_at[j], q_at[j], k_at[j], HALF)

    for h in range(width):
        cols = slice(h * NOPE, (h + 1) * NOPE)
        for start in range(0, HALF, CHUNK):
            rows = slice(start, start + CHUNK)
            row = lax.broadcasted_iota(jnp.int32, (CHUNK, HALF), 0) + start
            causal = lax.broadcasted_iota(jnp.int32, (CHUNK, HALF), 1) <= row
            late = [score_s[h, rows, i * HALF : (i + 1) * HALF] for i in range(STEPS + 1)]
            late[STEPS] = jnp.where(causal, late[STEPS], NEG)
            first = jnp.where(causal, score_s[h, rows, full : full + HALF], NEG)
            chosen = [score_s[h, rows, at : at + HALF] for at in chosen_at]
            top_late = functools.reduce(jnp.maximum, late)
            top_first = first
            for e, s in zip(early, chosen):
                top_late = jnp.maximum(top_late, jnp.where(e, NEG, s))
                top_first = jnp.maximum(top_first, jnp.where(e, s, NEG))
            top_late = jnp.max(top_late, axis=1, keepdims=True)
            top_first = jnp.max(top_first, axis=1, keepdims=True)
            sum_late = jnp.zeros((CHUNK, HALF), jnp.float32)
            for i, s in enumerate(late):
                p = jnp.exp2((s - top_late) * coef)
                sum_late = sum_late + p
                prob_s[h, rows, i * HALF : (i + 1) * HALF] = p.astype(jnp.bfloat16)
            p = jnp.exp2((first - top_first) * coef)
            sum_first = p
            prob_s[h, rows, full : full + HALF] = p.astype(jnp.bfloat16)
            for e, s, at in zip(early, chosen, chosen_at):
                p = jnp.exp2((s - jnp.where(e, top_first, top_late)) * coef)
                sum_late = sum_late + jnp.where(e, 0.0, p)
                sum_first = sum_first + jnp.where(e, p, 0.0)
                prob_s[h, rows, at : at + HALF] = p.astype(jnp.bfloat16)
            sum_s[h, 0, rows, :] = jnp.sum(sum_late, axis=1, keepdims=True)
            sum_s[h, 1, rows, :] = jnp.sum(sum_first, axis=1, keepdims=True)

        def weighted(at, k_start, count):
            return jnp.dot(
                prob_s[h, :, at : at + count],
                val_s[pl.ds(k_start, count), cols],
                preferred_element_type=jnp.float32,
            )

        out_late = weighted(0, 0, full)
        out_first = weighted(full, 0, HALF)
        for j, e in enumerate(early):
            part = weighted(chosen_at[j], k_at[j], HALF)
            out_late = out_late + jnp.where(e, 0.0, part)
            out_first = out_first + jnp.where(e, part, 0.0)
        o_ref[:HALF, cols] = (out_first / sum_s[h, 1]).astype(jnp.bfloat16)
        o_ref[HALF:, cols] = (out_late / sum_s[h, 0]).astype(jnp.bfloat16)


def attend(first, heads, sel, lat, rot, q_nope, q_rot, weights, earlier):
    tok_len, all_cols = q_nope.shape
    width = 4
    cols = width * NOPE
    steps = heads // width
    count, depth = lat.shape
    blocks = 2 * STEPS + 1

    def whole(shape):
        return pl.BlockSpec(shape, lambda i: (0, 0))

    def mine(shape):
        return pl.BlockSpec(shape, lambda i: (0, first // width + i))

    in_specs = [
        pl.BlockSpec(memory_space=pltpu.SMEM),
        whole(lat.shape),
        whole(rot.shape),
        mine((tok_len, cols)),
        mine((tok_len, cols)),
    ]
    in_specs += [pl.BlockSpec((w.shape[0], cols), lambda i: (0, i)) for w in weights]
    in_specs += [pl.BlockSpec((w.shape[0], cols), lambda i: (0, steps + i)) for w in weights]
    operands = [sel, lat, rot, q_nope, q_rot, *weights, *weights]
    aliases = {}
    if earlier is not None:
        in_specs.append(pl.BlockSpec(memory_space=pl.ANY))
        aliases = {len(operands): 0}
        operands.append(earlier)
    some = heads * NOPE
    flops = 4 * count * depth * some + heads * blocks * HALF * HALF * (2 * 256 + 2 * VDIM)
    return pl.pallas_call(
        functools.partial(attend_kernel, width),
        grid=(steps,),
        in_specs=in_specs,
        out_specs=mine((tok_len, cols)),
        out_shape=jax.ShapeDtypeStruct((tok_len, all_cols), jnp.bfloat16),
        scratch_shapes=[
            pltpu.VMEM((count, cols), jnp.bfloat16),
            pltpu.VMEM((count, cols), jnp.bfloat16),
            pltpu.VMEM((width, HALF, blocks * HALF), jnp.float32),
            pltpu.VMEM((width, HALF, blocks * HALF), jnp.bfloat16),
            pltpu.VMEM((width, 2, HALF, 1), jnp.float32),
        ],
        input_output_aliases=aliases,
        compiler_params=pltpu.CompilerParams(vmem_limit_bytes=40 * 1024 * 1024),
        cost_estimate=pl.CostEstimate(
            flops=flops,
            bytes_accessed=2 * (4 * depth * some + 3 * tok_len * some + count * 640),
            transcendentals=heads * blocks * HALF * HALF,
        ),
        name=f"attend_{first}",
    )(*operands)


def local(q_nope, q_rope, latent, k_rope, blocks, w_uk, w_uv):
    w_rows = w_uk.shape[0]
    parts = [(0, 12), (12, 4)]
    n_ctx = lax.axis_size("ctx")
    ctx_index = lax.axis_index("ctx")
    head_index = lax.axis_index("head")
    z, x = ctx_index // (NX * NY), (ctx_index // NY) % NX
    own = jnp.concatenate([latent, k_rope, k_rope], 1)
    visited = [own]
    for step in range(1, STEPS):
        pairs = [(source, (source + step) % n_ctx) for source in range(n_ctx)]
        visited.append(lax.ppermute(own, "ctx", pairs))
    held = jnp.stack(visited)

    own_rows = gather_own(
        jnp.concatenate([w[:, f * NOPE : (f + n) * NOPE] for f, n in parts for w in (w_uk, w_uv)], 1)
    )

    shards = (ctx_index - jnp.arange(STEPS, dtype=jnp.int32)) % n_ctx
    at = jnp.arange(n_ctx, dtype=jnp.int32)[:, None] == shards[None, :]
    pairs_of = jnp.sum(jnp.where(at[:, None, :], blocks[:, :, None], 0), axis=0)
    rows = jnp.arange(HALF, dtype=jnp.int32)
    pos = (pairs_of[:, :, None] * HALF + rows).reshape(-1)
    half = ROPE // 2
    freq = 10000.0 ** (-(2.0 * jnp.arange(half, dtype=jnp.float32)) / ROPE)
    angles = pos.astype(jnp.float32)[None, :] * freq[:, None]
    cosine, sine = jnp.cos(angles), jnp.sin(angles)
    q_rot = rotate_queries(q_rope, cosine, sine)
    sel = (pairs_of[0, 1:] < pairs_of[0, 0]).astype(jnp.int32)

    across = lax.ppermute(held, "head", [(0, 2), (2, 0), (1, 3), (3, 1)])
    upper = head_index // 2 == 0
    zero = q_rot[0, 0] * 0
    weights = []
    for i, (first, count) in enumerate(parts):
        cols = slice(2 * first * NOPE, 2 * (first + count) * NOPE)
        weights.append(gather_rest(own_rows[:, cols] + zero, 1 - 2 * i))
    two = jnp.stack([jnp.where(upper, held, across), jnp.where(upper, across, held)])
    both = lax.all_gather(two, "head", axis=0, axis_index_groups=[[0, 1], [2, 3]])
    order = row_order(plan_of(head_index), z, x, w_rows)
    lat, rot = prepare_keys(both, order, cosine, sine)
    result = None
    for (first, count), some in zip(parts, weights):
        result = attend(first, count, sel, lat, rot, q_nope, q_rot, some, result)
    return result


def solution(mesh):
    in_specs = (
        P("ctx", "head"),
        P("ctx", "head"),
        P(("ctx", "head"), None),
        P(("ctx", "head"), None),
        P(),
        P("ctx", "head"),
        P("ctx", "head"),
    )
    out_specs = P("ctx", "head")
    return jax.shard_map(local, mesh=mesh, in_specs=in_specs, out_specs=out_specs, check_vma=False)
```

```python
import functools

import jax
import jax.numpy as jnp
from jax import lax
from jax.experimental import pallas as pl
from jax.experimental.pallas import tpu as pltpu
from jax.sharding import PartitionSpec as P

ROPE = 64
NOPE = 128
VDIM = 128
STEPS = 3
NZ, NX, NY = 8, 4, 4
N_HEAD = 4
HALF = 128
CHUNK = 32
LOG2E = 1.4426950408889634
NEG = -1e30


def place(z, x, y):
    return ((z % NZ) * NX + x % NX) * NY + y


def members(plan, colour):
    if plan == 0:
        return [(z, (colour - 2 * z) % NX) for z in range(NZ)]
    return [((colour - 2 * x) % 4 + 4 * far, x) for x in range(NX) for far in range(2)]


def plan_of(head):
    return head % 2


def colour_of(plan, z, x):
    return jnp.where(plan == 0, x + 2 * z, z + 2 * x) % 4


def spread(value, groups):
    size = len(groups[0])
    return lax.all_to_all(
        jnp.broadcast_to(value[None], (size,) + value.shape),
        ("ctx", "head"),
        0,
        0,
        axis_index_groups=groups,
    ).reshape(size * value.shape[0], value.shape[1])


def gather_own(shard):
    lines = [
        [place(z, x, y) * N_HEAD + head for y in range(NY)]
        for head in range(N_HEAD)
        for z in range(NZ)
        for x in range(NX)
    ]
    colours = [
        [place(z, x, y) * N_HEAD + head for z, x in members(plan_of(head), c)]
        for head in range(N_HEAD)
        for c in range(4)
        for y in range(NY)
    ]
    return spread(spread(shard, lines), colours)


def from_neighbour(value, step, along):
    pairs = []
    for head in range(N_HEAD):
        on_x = (plan_of(head) == 0) == (along == 0)
        dz, dx = (0, step) if on_x else (step, 0)
        pairs += [
            (place(z + dz, x + dx, y) * N_HEAD + head, place(z, x, y) * N_HEAD + head)
            for z in range(NZ)
            for x in range(NX)
            for y in range(NY)
        ]
    return lax.ppermute(value, ("ctx", "head"), pairs)


def gather_rest(own, side):
    return own, from_neighbour(own, 1, 0), from_neighbour(own, -1, 0), from_neighbour(own, side, 1)


def row_order(plan, z, x, rows):
    at = jnp.arange(NZ * NX * NY * rows, dtype=jnp.int32)
    quarter = at.shape[0] // 4
    piece, rest = at // quarter, at % quarter
    step = jnp.where(piece < 2, piece, 5 - piece)
    colour = (colour_of(plan, z, x) + step) % 4
    member, inner = rest // (NY * rows), rest % (NY * rows)
    mz = jnp.where(plan == 0, member, (colour - 2 * (member // 2)) % 4 + 4 * (member % 2))
    mx = jnp.where(plan == 0, (colour - 2 * member) % 4, member // 2)
    return (mz * NX + mx) * (NY * rows) + inner


def factors(cosine, sine):
    return (
        jnp.concatenate([cosine] * 4, 0).T,
        jnp.concatenate([-sine, sine, -sine, sine], 0).T,
    )


def turned(x, cosine, sine):
    lane = lax.broadcasted_iota(jnp.int32, x.shape, 1)
    swapped = jnp.where(lane % 64 < 32, pltpu.roll(x, 96, 1), pltpu.roll(x, 32, 1))
    return x * cosine + swapped * sine


def rotate_queries_kernel(x_ref, cos_ref, sin_ref, o_ref, cos_s, sin_s):
    rows = x_ref.shape[0]
    left = lax.broadcasted_iota(jnp.int32, (rows, 128), 1) < 64

    @pl.when(pl.program_id(0) == 0)
    def _():
        def own(ref):
            late = STEPS * HALF
            return jnp.concatenate([ref[:, :HALF], ref[:, late : late + HALF]], 1)

        cos_s[...], sin_s[...] = factors(own(cos_ref), own(sin_ref))

    cosine, sine = cos_s[...], sin_s[...]
    for pair in range(x_ref.shape[1] // 128):
        x = turned(x_ref[:, pair * 128 : (pair + 1) * 128].astype(jnp.float32), cosine, sine)
        high = x.astype(jnp.bfloat16).astype(jnp.float32)
        rest = x - high
        first = jnp.where(left, high, pltpu.roll(rest, 64, 1))
        second = jnp.where(left, pltpu.roll(high, 64, 1), rest)
        o_ref[:, pair * 256 : pair * 256 + 128] = first.astype(jnp.bfloat16)
        o_ref[:, pair * 256 + 128 : pair * 256 + 256] = second.astype(jnp.bfloat16)


def rotate_queries(q_rope, cosine, sine):
    tok_len, width = q_rope.shape
    return pl.pallas_call(
        rotate_queries_kernel,
        grid=(4,),
        in_specs=[
            pl.BlockSpec((tok_len, width // 4), lambda i: (0, i)),
            pl.BlockSpec(cosine.shape, lambda i: (0, 0)),
            pl.BlockSpec(sine.shape, lambda i: (0, 0)),
        ],
        out_specs=pl.BlockSpec((tok_len, width // 2), lambda i: (0, i)),
        out_shape=jax.ShapeDtypeStruct((tok_len, 2 * width), jnp.bfloat16),
        scratch_shapes=[pltpu.VMEM((tok_len, 128), jnp.float32)] * 2,
        cost_estimate=pl.CostEstimate(
            flops=4 * tok_len * width, bytes_accessed=6 * tok_len * width, transcendentals=0
        ),
        name="rotate_queries",
    )(q_rope, cosine, sine)


def prepare_keys_kernel(held_ref, order_ref, cos_ref, sin_ref, lat_ref, rot_ref):
    cores, halves, steps, _, _ = held_ref.shape
    depth = lat_ref.shape[1]
    held = jnp.concatenate(
        [
            held_ref[core, half, step]
            for half in range(halves)
            for step in range(steps)
            for core in range(cores)
        ],
        0,
    )
    at = lax.broadcasted_iota(jnp.int32, (depth, depth), 0)
    place_of = (at == order_ref[...]).astype(jnp.float32).astype(jnp.bfloat16)
    lat = jnp.dot(held[:, :depth], place_of, preferred_element_type=jnp.float32)
    lat_ref[...] = lat.astype(jnp.bfloat16)
    rot = turned(held[:, depth:].astype(jnp.float32), *factors(cos_ref[...], sin_ref[...]))
    rot_ref[...] = rot.astype(jnp.bfloat16)


def prepare_keys(held, order, cosine, sine):
    depth = order.shape[0]
    count = cosine.shape[1]
    return pl.pallas_call(
        prepare_keys_kernel,
        out_shape=(
            jax.ShapeDtypeStruct((count, depth), jnp.bfloat16),
            jax.ShapeDtypeStruct((count, 128), jnp.bfloat16),
        ),
        cost_estimate=pl.CostEstimate(
            flops=2 * count * depth * depth, bytes_accessed=6 * count * 640, transcendentals=0
        ),
        compiler_params=pltpu.CompilerParams(vmem_limit_bytes=32 * 1024 * 1024),
        name="prepare_keys",
    )(held, order[None, :], cosine, sine)


def attend_kernel(width, sel_ref, lat_ref, rot_ref, qn_ref, qr_ref, *refs):
    o_ref, key_s, val_s, score_s, prob_s, sum_s = refs[-6:]
    lat = lat_ref[...]
    pieces = 4
    up_k = jnp.concatenate([r[...] for r in refs[:pieces]], 0)
    up_v = jnp.concatenate([r[...] for r in refs[pieces : 2 * pieces]], 0)
    key_s[...] = jnp.dot(lat, up_k, preferred_element_type=jnp.float32).astype(jnp.bfloat16)
    val_s[...] = jnp.dot(lat, up_v, preferred_element_type=jnp.float32).astype(jnp.bfloat16)
    coef = LOG2E / (NOPE + ROPE) ** 0.5
    contract = (((1,), (1,)), ((), ()))
    early = [sel_ref[j] != 0 for j in range(STEPS - 1)]
    q_at = [pl.multiple_of(jnp.where(e, 0, HALF), HALF) for e in early]
    k_at = [
        pl.multiple_of(jnp.where(e, j + 1, STEPS + j + 1) * HALF, HALF)
        for j, e in enumerate(early)
    ]
    full = (STEPS + 1) * HALF
    chosen_at = [full + (j + 1) * HALF for j in range(STEPS - 1)]

    for h in range(width):
        cols = slice(h * NOPE, (h + 1) * NOPE)

        def scores(at, q_start, k_start, count):
            q_rows, k_rows = pl.ds(q_start, HALF), pl.ds(k_start, count)
            q = jnp.concatenate([qn_ref[q_rows, cols], qr_ref[q_rows, cols]], 1)
            k = jnp.concatenate([key_s[k_rows, cols], rot_ref[k_rows, :]], 1)
            score_s[h, :, at : at + count] = lax.dot_general(
                q, k, contract, preferred_element_type=jnp.float32
            )

        scores(0, HALF, 0, full)
        scores(full, 0, 0, HALF)
        for j in range(STEPS - 1):
            scores(chosen_at[j], q_at[j], k_at[j], HALF)

    for h in range(width):
        cols = slice(h * NOPE, (h + 1) * NOPE)
        for start in range(0, HALF, CHUNK):
            rows = slice(start, start + CHUNK)
            row = lax.broadcasted_iota(jnp.int32, (CHUNK, HALF), 0) + start
            causal = lax.broadcasted_iota(jnp.int32, (CHUNK, HALF), 1) <= row
            late = [score_s[h, rows, i * HALF : (i + 1) * HALF] for i in range(STEPS + 1)]
            late[STEPS] = jnp.where(causal, late[STEPS], NEG)
            first = jnp.where(causal, score_s[h, rows, full : full + HALF], NEG)
            chosen = [score_s[h, rows, at : at + HALF] for at in chosen_at]
            top_late = functools.reduce(jnp.maximum, late)
            top_first = first
            for e, s in zip(early, chosen):
                top_late = jnp.maximum(top_late, jnp.where(e, NEG, s))
                top_first = jnp.maximum(top_first, jnp.where(e, s, NEG))
            top_late = jnp.max(top_late, axis=1, keepdims=True)
            top_first = jnp.max(top_first, axis=1, keepdims=True)
            sum_late = jnp.zeros((CHUNK, HALF), jnp.float32)
            for i, s in enumerate(late):
                p = jnp.exp2((s - top_late) * coef)
                sum_late = sum_late + p
                prob_s[h, rows, i * HALF : (i + 1) * HALF] = p.astype(jnp.bfloat16)
            p = jnp.exp2((first - top_first) * coef)
            sum_first = p
            prob_s[h, rows, full : full + HALF] = p.astype(jnp.bfloat16)
            for e, s, at in zip(early, chosen, chosen_at):
                p = jnp.exp2((s - jnp.where(e, top_first, top_late)) * coef)
                sum_late = sum_late + jnp.where(e, 0.0, p)
                sum_first = sum_first + jnp.where(e, p, 0.0)
                prob_s[h, rows, at : at + HALF] = p.astype(jnp.bfloat16)
            sum_s[h, 0, rows, :] = jnp.sum(sum_late, axis=1, keepdims=True)
            sum_s[h, 1, rows, :] = jnp.sum(sum_first, axis=1, keepdims=True)

        def weighted(at, k_start, count):
            return jnp.dot(
                prob_s[h, :, at : at + count],
                val_s[pl.ds(k_start, count), cols],
                preferred_element_type=jnp.float32,
            )

        out_late = weighted(0, 0, full)
        out_first = weighted(full, 0, HALF)
        for j, e in enumerate(early):
            part = weighted(chosen_at[j], k_at[j], HALF)
            out_late = out_late + jnp.where(e, 0.0, part)
            out_first = out_first + jnp.where(e, part, 0.0)
        o_ref[:HALF, cols] = (out_first / sum_s[h, 1]).astype(jnp.bfloat16)
        o_ref[HALF:, cols] = (out_late / sum_s[h, 0]).astype(jnp.bfloat16)


def attend(first, heads, sel, lat, rot, q_nope, q_rot, weights, earlier):
    tok_len, all_cols = q_nope.shape
    width = 6 if heads % 6 == 0 and first % 6 == 0 else 4
    cols = width * NOPE
    steps = heads // width
    count, depth = lat.shape
    blocks = 2 * STEPS + 1

    def whole(shape):
        return pl.BlockSpec(shape, lambda i: (0, 0))

    def mine(shape):
        return pl.BlockSpec(shape, lambda i: (0, first // width + i))

    in_specs = [
        pl.BlockSpec(memory_space=pltpu.SMEM),
        whole(lat.shape),
        whole(rot.shape),
        mine((tok_len, cols)),
        mine((tok_len, cols)),
    ]
    in_specs += [pl.BlockSpec((w.shape[0], cols), lambda i: (0, i)) for w in weights]
    in_specs += [pl.BlockSpec((w.shape[0], cols), lambda i: (0, steps + i)) for w in weights]
    operands = [sel, lat, rot, q_nope, q_rot, *weights, *weights]
    aliases = {}
    if earlier is not None:
        in_specs.append(pl.BlockSpec(memory_space=pl.ANY))
        aliases = {len(operands): 0}
        operands.append(earlier)
    some = heads * NOPE
    flops = 4 * count * depth * some + heads * blocks * HALF * HALF * (2 * 256 + 2 * VDIM)
    return pl.pallas_call(
        functools.partial(attend_kernel, width),
        grid=(steps,),
        in_specs=in_specs,
        out_specs=mine((tok_len, cols)),
        out_shape=jax.ShapeDtypeStruct((tok_len, all_cols), jnp.bfloat16),
        scratch_shapes=[
            pltpu.VMEM((count, cols), jnp.bfloat16),
            pltpu.VMEM((count, cols), jnp.bfloat16),
            pltpu.VMEM((width, HALF, blocks * HALF), jnp.float32),
            pltpu.VMEM((width, HALF, blocks * HALF), jnp.bfloat16),
            pltpu.VMEM((width, 2, HALF, 1), jnp.float32),
        ],
        input_output_aliases=aliases,
        compiler_params=pltpu.CompilerParams(vmem_limit_bytes=40 * 1024 * 1024),
        cost_estimate=pl.CostEstimate(
            flops=flops,
            bytes_accessed=2 * (4 * depth * some + 3 * tok_len * some + count * 640),
            transcendentals=heads * blocks * HALF * HALF,
        ),
        name=f"attend_{first}",
    )(*operands)


def local(q_nope, q_rope, latent, k_rope, blocks, w_uk, w_uv):
    w_rows = w_uk.shape[0]
    parts = [(0, 12), (12, 4)]
    n_ctx = lax.axis_size("ctx")
    ctx_index = lax.axis_index("ctx")
    head_index = lax.axis_index("head")
    z, x = ctx_index // (NX * NY), (ctx_index // NY) % NX
    own = jnp.concatenate([latent, k_rope, k_rope], 1)
    visited = [own]
    for step in range(1, STEPS):
        pairs = [(source, (source + step) % n_ctx) for source in range(n_ctx)]
        visited.append(lax.ppermute(own, "ctx", pairs))
    held = jnp.stack(visited)

    own_rows = gather_own(
        jnp.concatenate([w[:, f * NOPE : (f + n) * NOPE] for f, n in parts for w in (w_uk, w_uv)], 1)
    )

    shards = (ctx_index - jnp.arange(STEPS, dtype=jnp.int32)) % n_ctx
    at = jnp.arange(n_ctx, dtype=jnp.int32)[:, None] == shards[None, :]
    pairs_of = jnp.sum(jnp.where(at[:, None, :], blocks[:, :, None], 0), axis=0)
    rows = jnp.arange(HALF, dtype=jnp.int32)
    pos = (pairs_of[:, :, None] * HALF + rows).reshape(-1)
    half = ROPE // 2
    freq = 10000.0 ** (-(2.0 * jnp.arange(half, dtype=jnp.float32)) / ROPE)
    angles = pos.astype(jnp.float32)[None, :] * freq[:, None]
    cosine, sine = jnp.cos(angles), jnp.sin(angles)
    q_rot = rotate_queries(q_rope, cosine, sine)
    sel = (pairs_of[0, 1:] < pairs_of[0, 0]).astype(jnp.int32)

    across = lax.ppermute(held, "head", [(0, 2), (2, 0), (1, 3), (3, 1)])
    upper = head_index // 2 == 0
    zero = q_rot[0, 0] * 0
    weights = []
    for i, (first, count) in enumerate(parts):
        cols = slice(2 * first * NOPE, 2 * (first + count) * NOPE)
        weights.append(gather_rest(own_rows[:, cols] + zero, 1 - 2 * i))
    two = jnp.stack([jnp.where(upper, held, across), jnp.where(upper, across, held)])
    both = lax.all_gather(two, "head", axis=0, axis_index_groups=[[0, 1], [2, 3]])
    order = row_order(plan_of(head_index), z, x, w_rows)
    lat, rot = prepare_keys(both, order, cosine, sine)
    result = None
    for (first, count), some in zip(parts, weights):
        result = attend(first, count, sel, lat, rot, q_nope, q_rot, some, result)
    return result


def solution(mesh):
    in_specs = (
        P("ctx", "head"),
        P("ctx", "head"),
        P(("ctx", "head"), None),
        P(("ctx", "head"), None),
        P(),
        P("ctx", "head"),
        P("ctx", "head"),
    )
    out_specs = P("ctx", "head")
    return jax.shard_map(local, mesh=mesh, in_specs=in_specs, out_specs=out_specs, check_vma=False)
```
